32 devices in a mesh: dp: 8 (over z, core), seq: 4 (over y, x).
Axes of the slice: x: 2, y: 2, z: 4, core: 2. Of those that a mesh axis runs over, the one named last changes fastest.
Arguments:
- tokens: bfloat16 [8, 2048, 1024], P('dp', 'seq'), may hold values from -6 to 6
- input_weight: bfloat16 [1024, 3072], P(('dp', 'seq')), may hold values from -0.1875 to 0.1875
- input_bias: bfloat16 [3072], P(('dp', 'seq')), may hold values from -1.75 to 1.75
- output_weight: bfloat16 [1024, 1024], P(('dp', 'seq')), may hold values from -4 to 4
- output_bias: bfloat16 [1024], P(('dp', 'seq')), may hold values from -1.75 to 1.75
- up_weight: bfloat16 [1024, 4096], P(('dp', 'seq')), may hold values from -0.1875 to 0.1875
- up_bias: bfloat16 [4096], P(('dp', 'seq')), may hold values from -1.75 to 1.75
- down_weight: bfloat16 [4096, 1024], P(('dp', 'seq')), may hold values from -0.09375 to 0.09375
- down_bias: bfloat16 [1024], P(('dp', 'seq')), may hold values from -1.75 to 1.75
- attention_gain: bfloat16 [1024], P(('dp', 'seq')), may hold values from 0.099609375 to 1.8984375
- attention_shift: bfloat16 [1024], P(('dp', 'seq')), may hold values from -1.75 to 1.75
- feedforward_gain: bfloat16 [1024], P(('dp', 'seq')), may hold values from 0.099609375 to 1.8984375
- feedforward_shift: bfloat16 [1024], P(('dp', 'seq')), may hold values from -1.75 to 1.75
- cotangent: bfloat16 [8, 2048, 1024], P('dp', 'seq'), may hold values from -6 to 6
Outputs:
- output: bfloat16 [8, 2048, 1024], P('dp', 'seq')
- token_grad: bfloat16 [8, 2048, 1024], P('dp', 'seq')
- input_weight_grad: float32 [1024, 3072], P(('dp', 'seq'))
- input_bias_grad: float32 [2048], P(('dp', 'seq'))
- value_bias_grad: float32 [1024], P(('dp', 'seq'))
- output_weight_grad: float32 [1024, 1024], P(('dp', 'seq'))
- output_bias_grad: float32 [1024], P(('dp', 'seq'))
- up_weight_grad: float32 [1024, 4096], P(('dp', 'seq'))
- up_bias_grad: float32 [4096], P(('dp', 'seq'))
- down_weight_grad: float32 [4096, 1024], P(('dp', 'seq'))
- down_bias_grad: float32 [1024], P(('dp', 'seq'))
- attention_gain_grad: float32 [1024], P(('dp', 'seq'))
- attention_shift_grad: float32 [1024], P(('dp', 'seq'))
- feedforward_gain_grad: float32 [1024], P(('dp', 'seq'))
- feedforward_shift_grad: float32 [1024], P(('dp', 'seq'))
The draws below stay inside these ranges and needn't reach their ends.
All inputs are finite; a program needn't handle non-finite values.
Results may differ from the reference program's by a relative error of at most 0.014.
Values may be sent and summed in bfloat16 or wider, within the bound.
No kernel may reach another device: no remote copies, remote signals or barrier semaphores. Data moves between devices by JAX's collectives and lax.ppermute only.
A program may use at most 256 MiB of HBM per device.

```python
import math
import jax
import jax.numpy as jnp
from jax import lax

D = 1024
HEADS = 16
FF = 4096
HEAD_DIM = 64
ROT = 16
LENGTH = 2048
SEQUENCES = 8
TOKENS = 16384


def level_of(key, extent, split, smallest, top_value):
    def one(position, shards_of):
        draws = jax.random.uniform(jax.random.fold_in(jax.random.fold_in(key, 6), position), (shards_of,), jnp.float32, smallest / len(split), top_value / len(split))
        return jnp.repeat(jnp.exp(draws), extent[position] // shards_of).reshape((-1,) + (1,) * (len(extent) - position - 1))

    loudness = one(*split[0])
    for cut in split[1:]:
        loudness = loudness * one(*cut)
    return loudness


def bell_draw(rng, extent, width, reach, split=(), kind=jnp.bfloat16):
    values = jax.random.normal(rng, extent, jnp.float32) * width
    if len(split) > 0:
        values = level_of(rng, extent, split, -0.22, 0.18) * values
    return jnp.clip(values, min=-reach, max=reach).astype(kind)


def setup_inputs(seed: int = 0) -> dict:
    key_list = jax.random.split(jax.random.key(seed), 15)
    return {
        "tokens": bell_draw(key_list[0], (SEQUENCES, LENGTH, D), 1.0, 6.0, ((0, 8), (1, 4))),
        "input_weight": bell_draw(key_list[1], (D, 3 * D), D ** -0.5, 0.1875, ((0, 32),)),
        "input_bias": bell_draw(key_list[2], (3 * D,), 0.3, 1.75, ((0, 32),)),
        "output_weight": bell_draw(key_list[3], (D, D), (max(1, D * 4 // LENGTH)) ** -0.5, 4.0, ((0, 32),)),
        "output_bias": bell_draw(key_list[4], (D,), 0.3, 1.75, ((0, 32),)),
        "up_weight": bell_draw(key_list[5], (D, FF), D ** -0.5, 0.1875, ((0, 32),)),
        "up_bias": bell_draw(key_list[6], (FF,), 0.3, 1.75, ((0, 32),)),
        "down_weight": bell_draw(key_list[7], (FF, D), FF ** -0.5, 0.09375, ((0, 32),)),
        "down_bias": bell_draw(key_list[8], (D,), 0.3, 1.75, ((0, 32),)),
        "attention_gain": jnp.clip(1.0 + 0.18 * jax.random.normal(key_list[9], (D,), jnp.float32), 0.099609375, 1.8984375).astype(jnp.bfloat16),
        "attention_shift": bell_draw(key_list[10], (D,), 0.3, 1.75, ((0, 32),)),
        "feedforward_gain": jnp.clip(1.0 + 0.18 * jax.random.normal(key_list[11], (D,), jnp.float32), 0.099609375, 1.8984375).astype(jnp.bfloat16),
        "feedforward_shift": bell_draw(key_list[12], (D,), 0.3, 1.75, ((0, 32),)),
        "cotangent": bell_draw(key_list[13], (SEQUENCES, LENGTH, D), 1.0, 6.0, ((0, 8), (1, 4))),
    }


@jax.custom_vjp
def low(v):
    return lax.optimization_barrier(v.astype(jnp.bfloat16)).astype(jnp.float32)

@jax.custom_vjp
def low_back(v):
    return v

def low_keep(v):
    return (low(v), None)

def low_pass(kept, grad):
    return (grad,)

def back_keep(v):
    return (v, None)

def back_low(kept, grad):
    return (low(grad),)
low.defvjp(low_keep, low_pass)
low_back.defvjp(back_keep, back_low)
norm_eps = 1e-05
masked_score = -1e+30
highest = lax.Precision.HIGHEST

def layer_norm(inputs, gain, shift):
    centered = inputs - lax.optimization_barrier(jnp.mean(inputs, axis=-1, keepdims=True))
    variance = lax.optimization_barrier(jnp.mean(centered * centered, axis=-1, keepdims=True))
    return centered * lax.rsqrt(variance + norm_eps) * gain + shift

def rotary_tables(positions, rotary_dims):
    exponent = -jnp.arange(0, rotary_dims, 2, dtype=jnp.float32) / rotary_dims
    frequency = jnp.float32(10000.0) ** exponent
    phase = positions.astype(jnp.float32)[:, None] * frequency[None, :]
    phase = jnp.concatenate([phase, phase], axis=-1)
    return (jnp.cos(phase), jnp.sin(phase))

def rotate(inputs, cosine, sine):
    rotary_dims = cosine.shape[-1]
    half = rotary_dims // 2
    front = inputs[..., :rotary_dims]
    turned = jnp.concatenate([-front[..., half:], front[..., :half]], axis=-1)
    front = front * cosine[:, None, :] + turned * sine[:, None, :]
    return jnp.concatenate([front, inputs[..., rotary_dims:]], axis=-1)

def attention_block(query_block, query_start, key_seq, value_seq):
    block_rows = query_block.shape[0]
    scores = jnp.einsum('qhe,khe->hqk', query_block, key_seq, precision=highest) / math.sqrt(HEAD_DIM)
    scores = low_back(scores)
    query_pos = query_start + jnp.arange(block_rows, dtype=jnp.int32)
    key_pos = jnp.arange(key_seq.shape[0], dtype=jnp.int32)
    allowed = key_pos[None, None, :] <= query_pos[None, :, None]
    scores = jnp.where(allowed, scores, masked_score)
    highest_score = lax.optimization_barrier(jnp.max(scores, axis=-1, keepdims=True))
    logsum = jnp.log(lax.optimization_barrier(jnp.sum(jnp.exp(scores - highest_score), axis=-1, keepdims=True))) + highest_score
    probs = low(jnp.exp(scores - logsum))
    return jnp.einsum('hqk,khe->qhe', probs, value_seq, precision=highest)

def sequence_attention(item):
    query_seq, key_seq, value_seq = item
    block = math.gcd(LENGTH, 512)
    count = LENGTH // block
    query_blocks = query_seq.reshape(count, block, HEADS, HEAD_DIM)
    starts = jnp.arange(count, dtype=jnp.int32) * block

    def one_block(pair):
        return attention_block(pair[0], pair[1], key_seq, value_seq)
    results = lax.map(jax.checkpoint(one_block), (query_blocks, starts))
    return results.reshape(LENGTH, HEADS, HEAD_DIM)

def forward(tokens, input_weight, input_bias, output_weight, output_bias, up_weight, up_bias, down_weight, down_bias, attention_gain, attention_shift, feedforward_gain, feedforward_shift):
    flat = tokens.reshape(TOKENS, D)
    normed_attn = low(layer_norm(flat, attention_gain, attention_shift))
    mixed = low_back(jnp.dot(normed_attn, input_weight, precision=highest) + input_bias)
    mixed = mixed.reshape(SEQUENCES, LENGTH, 3, HEADS, HEAD_DIM)
    cosine, sine = rotary_tables(jnp.arange(LENGTH, dtype=jnp.int32), ROT)
    queries = low(low_back(rotate(mixed[:, :, 0], cosine, sine)))
    keys = low(low_back(rotate(mixed[:, :, 1], cosine, sine)))
    values = low(mixed[:, :, 2])
    attended = lax.map(sequence_attention, (queries, keys, values))
    attended = low(low_back(attended.reshape(TOKENS, D)))
    attention_out = jnp.dot(attended, output_weight, precision=highest) + output_bias
    normed_ff = low(layer_norm(flat, feedforward_gain, feedforward_shift))
    hidden = low_back(jnp.dot(normed_ff, up_weight, precision=highest) + up_bias)
    active = low(jax.nn.gelu(hidden, approximate=False))
    ff_out = jnp.dot(active, down_weight, precision=highest) + down_bias
    return (flat + attention_out + ff_out).reshape(SEQUENCES, LENGTH, D)

def reference(tokens, input_weight, input_bias, output_weight, output_bias, up_weight, up_bias, down_weight, down_bias, attention_gain, attention_shift, feedforward_gain, feedforward_shift, cotangent):
    floats = tuple((a.astype(jnp.float32) for a in (tokens, input_weight, input_bias, output_weight, output_bias, up_weight, up_bias, down_weight, down_bias, attention_gain, attention_shift, feedforward_gain, feedforward_shift)))
    output, pull = jax.vjp(forward, *floats)
    grads = pull(cotangent.astype(jnp.float32))
    return (output.astype(jnp.bfloat16), grads[0].astype(jnp.bfloat16), grads[1], grads[2][:2 * D], grads[2][2 * D:], grads[3], grads[4], grads[5], grads[6], grads[7], grads[8], grads[9], grads[10], grads[11], grads[12])
```

```python
import functools
import math

import jax
import jax.numpy as jnp
import numpy as np
from jax import lax
from jax.experimental import pallas as pl
from jax.experimental.pallas import tpu as pltpu
from jax.sharding import PartitionSpec as P

HEADS = 16
ROT = 16

norm_eps = 1e-05
masked_score = -1e30
low = jnp.bfloat16
full = jnp.float32
kernel_memory = 56 * 1024 * 1024


def place_at(pieces, spots, axis):
    count = len(pieces)
    shape = list(pieces[0].shape)
    shape.insert(axis, count)
    held = jnp.zeros(shape, pieces[0].dtype)
    for piece, spot in zip(pieces, spots):
        held = lax.dynamic_update_index_in_dim(held, piece, spot, axis)
    return held


def pick(array, spot, axis):
    return lax.dynamic_index_in_dim(array, spot, axis, keepdims=False)


class Layout:
    def __init__(self):
        self.dp = lax.axis_size("dp")
        self.seq = lax.axis_size("seq")
        self.cores = 2 if self.dp % 2 == 0 else 1
        self.line = self.dp // self.cores
        place = lax.axis_index("dp")
        self.core = place % self.cores
        self.z = place // self.cores
        self.rank = lax.axis_index("seq")

    def seq_swap(self, array, k):
        return lax.ppermute(array, "seq", [(i, i ^ k) for i in range(self.seq)])

    def core_swap(self, array):
        return lax.ppermute(array, "dp", [(i, i ^ 1) for i in range(self.dp)])

    def z_shift(self, array, k):
        c = self.cores
        pairs = [(i, i + k * c) for i in range(self.dp) if 0 <= i + k * c < self.dp]
        return lax.ppermute(array, "dp", pairs)

    def z_turn(self, array, k):
        c = self.cores
        return lax.ppermute(array, "dp", [(i, (i + k * c) % self.dp) for i in range(self.dp)])

    def seq_exchange(self, piece_for):
        return [piece_for(self.rank)] + [
            self.seq_swap(piece_for(self.rank ^ k), k) for k in range(1, self.seq)
        ]

    def seq_spots(self):
        return [self.rank ^ k for k in range(self.seq)]

    def seq_gather(self, array):
        if self.seq != 4:
            return [array] + [self.seq_swap(array, k) for k in range(1, self.seq)]
        half = array.shape[1] // 2
        first, second = array[:, :half], array[:, half:]
        x_first = self.seq_swap(first, 1)
        y_second = self.seq_swap(second, 2)
        x_second = self.seq_swap(second, 1)
        y_first = self.seq_swap(first, 2)
        d_first = self.seq_swap(x_first, 2)
        d_second = self.seq_swap(y_second, 1)
        return [
            array,
            jnp.concatenate([x_first, x_second], 1),
            jnp.concatenate([y_first, y_second], 1),
            jnp.concatenate([d_first, d_second], 1),
        ]

    def seq_reduce(self, parts):
        if self.seq != 4:
            total = parts[0].astype(full)
            for k in range(1, self.seq):
                total = total + self.seq_swap(parts[k].astype(low), k).astype(full)
            return total
        half = parts[0].shape[1] // 2
        p1, p2, p3 = parts[1].astype(low), parts[2].astype(low), parts[3].astype(low)
        for_y = self.seq_swap(p3[:, :half], 1)
        for_x = self.seq_swap(p3[:, half:], 2)
        r1_first = self.seq_swap(p1[:, :half], 1)
        r2_second = self.seq_swap(p2[:, half:], 2)
        r1_second = self.seq_swap(
            (p1[:, half:].astype(full) + for_x.astype(full)).astype(low), 1
        )
        r2_first = self.seq_swap(
            (p2[:, :half].astype(full) + for_y.astype(full)).astype(low), 2
        )
        first = r1_first.astype(full) + r2_first.astype(full)
        second = r1_second.astype(full) + r2_second.astype(full)
        return parts[0].astype(full) + jnp.concatenate([first, second], 1)

    def dp_gather(self, array):
        right = left = array
        rights, lefts = [], []
        for _ in range(self.line - 1):
            right = self.z_shift(right, 1)
            left = self.z_shift(left, -1)
            rights.append(right)
            lefts.append(left)
        row = jnp.stack(rights[::-1] + [array] + lefts, 0)
        mine = lax.dynamic_slice_in_dim(row, self.line - 1 - self.z, self.line, 0)
        if self.cores == 1:
            return mine
        other = self.core_swap(mine)
        both = lax.dynamic_slice_in_dim(jnp.stack([mine, other, mine], 1), self.core, 2, 1)
        return both.reshape((self.dp,) + array.shape)

    def dp_reduce(self, array):
        if self.cores == 2:
            pairs = array.reshape((self.line, 2) + array.shape[1:])
            other = self.core_swap(pick(pairs, 1 - self.core, 1).astype(low))
            array = pick(pairs, self.core, 1).astype(full) + other.astype(full)

        def chunk(spot):
            return pick(array, jnp.clip(spot, 0, self.line - 1), 0)

        right = chunk(self.z + self.line - 1)
        left = chunk(self.z - self.line + 1)
        for step in range(1, self.line):
            far = self.line - 1 - step
            right = self.z_shift(right.astype(low), 1).astype(full)
            left = self.z_shift(left.astype(low), -1).astype(full)
            if far > 0:
                right = right + chunk(self.z + far)
                left = left + chunk(self.z - far)
        return chunk(self.z) + right + left

    def small_gather(self, vector):
        pieces = [vector] + [self.seq_swap(vector, k) for k in range(1, self.seq)]
        held = place_at(pieces, self.seq_spots(), 0)
        if self.cores == 2:
            held = place_at([held, self.core_swap(held)], [self.core, 1 - self.core], 0)
        else:
            held = held[None]
        pieces = [held] + [self.z_turn(held, k) for k in range(1, self.line)]
        spots = [(self.z - k) % self.line for k in range(self.line)]
        held = place_at(pieces, spots, 0)
        return held.reshape((self.dp, self.seq) + vector.shape)

    def small_reduce(self, array):
        array = sum(self.seq_exchange(lambda spot: pick(array, spot, 1)))
        if self.cores == 2:
            pairs = array.reshape((self.line, 2) + array.shape[1:])
            array = pick(pairs, self.core, 1) + self.core_swap(pick(pairs, 1 - self.core, 1))
        total = pick(array, self.z, 0)
        for k in range(1, self.line):
            total = total + self.z_turn(pick(array, (self.z + k) % self.line, 0), k)
        return total


def rotary_tables(length, lanes, head_dim):
    half = ROT // 2
    exponent = -np.arange(0, ROT, 2, dtype=np.float32) / np.float32(ROT)
    frequency = np.float32(10000.0) ** exponent
    phase = np.arange(length, dtype=np.float32)[:, None] * frequency[None, :]
    cosine = np.ones((length, head_dim), np.float32)
    sine = np.zeros((length, head_dim), np.float32)
    cosine[:, :half] = cosine[:, half:ROT] = np.cos(phase)
    sine[:, :half] = -np.sin(phase)
    sine[:, half:ROT] = np.sin(phase)
    copies = lanes // head_dim
    return np.tile(cosine, (1, copies)), np.tile(sine, (1, copies))


def roll_lanes(x, shift):
    size = x.shape[-1]
    if size % 128 == 0:
        return pltpu.roll(x, shift % size, x.ndim - 1)
    return jnp.roll(x, shift, -1)


def turn(x, cosine, sine, head_dim):
    half = ROT // 2
    lane = lax.broadcasted_iota(jnp.int32, x.shape, 1) % head_dim
    swapped = jnp.where(lane < half, roll_lanes(x, -half), roll_lanes(x, half))
    return x * cosine + swapped * sine


def normalised(x):
    mean = jnp.mean(x, axis=-1, keepdims=True)
    centered = x - mean
    variance = jnp.mean(centered * centered, axis=-1, keepdims=True)
    rstd = lax.rsqrt(variance + norm_eps)
    return centered * rstd, rstd


def project_kernel(head_dim, lanes, place, x_ref, weight_ref, bias_ref, norms_ref, cos_ref, sin_ref, attn_ref, ff_ref, qkv_ref):
    unit, _ = normalised(x_ref[...].astype(full))
    normed = (unit * norms_ref[0:1, :] + norms_ref[1:2, :]).astype(low)
    attn_ref[...] = normed
    ff_ref[...] = (unit * norms_ref[2:3, :] + norms_ref[3:4, :]).astype(low)
    mixed = jnp.dot(normed, weight_ref[...], preferred_element_type=full) + bias_ref[...]
    cosine, sine = cos_ref[...], sin_ref[...]
    for group in range(mixed.shape[1] // lanes):
        span = slice(group * lanes, (group + 1) * lanes)
        part = mixed[:, span]
        if group % 3 < 2:
            part = turn(part, cosine, sine, head_dim)
        qkv_ref[:, span] = part.astype(low)


def project(place, x, weight, bias, norms, cosine, sine, block, seqs, lanes, head_dim):
    rows, width = x.shape
    columns = weight.shape[1]
    whole = lambda i, place: (0, 0)
    step = lambda i, place: (i, 0)
    spot = lambda i, place: ((i // seqs) ^ place[0], 0)
    return pl.pallas_call(
        functools.partial(project_kernel, head_dim, lanes),
        grid_spec=pltpu.PrefetchScalarGridSpec(
            num_scalar_prefetch=1,
            grid=(rows // block,),
            in_specs=[
                pl.BlockSpec((block, width), step),
                pl.BlockSpec((width, columns), whole),
                pl.BlockSpec((1, columns), whole),
                pl.BlockSpec((4, width), whole),
                pl.BlockSpec((block, lanes), spot),
                pl.BlockSpec((block, lanes), spot),
            ],
            out_specs=[
                pl.BlockSpec((block, width), step),
                pl.BlockSpec((block, width), step),
                pl.BlockSpec((block, columns), step),
            ],
        ),
        out_shape=[
            jax.ShapeDtypeStruct((rows, width), low),
            jax.ShapeDtypeStruct((rows, width), low),
            jax.ShapeDtypeStruct((rows, columns), low),
        ],
        compiler_params=pltpu.CompilerParams(vmem_limit_bytes=kernel_memory),
        name="project",
    )(place, x, weight, bias, norms, cosine, sine)


def contract(a, b, da, db):
    return lax.dot_general(a, b, (((da,), (db,)), ((), ())), preferred_element_type=full)


def head_lanes(x, head, pair, head_dim):
    if pair == 1:
        return x
    lane = lax.broadcasted_iota(jnp.int32, x.shape, 1)
    inside = (lane >= head * head_dim) & (lane < (head + 1) * head_dim)
    return jnp.where(inside, x, jnp.zeros_like(x))


def attend_kernel(pair, head_dim, place, qkv_ref, exact_ref, low_ref, lse_ref):
    count, block, lanes3 = qkv_ref.shape
    lanes = lanes3 // 3
    scale = 1.0 / math.sqrt(head_dim)
    s = place[0]
    row = lax.broadcasted_iota(jnp.int32, (block, block), 0)
    column = lax.broadcasted_iota(jnp.int32, (block, block), 1)
    for i in range(count):
        here = i ^ s
        query = qkv_ref[here, :, 0:lanes] * jnp.asarray(scale, low)
        joined = jnp.zeros((block, lanes), full)
        for head in range(pair):
            mine = head_lanes(query, head, pair, head_dim)
            scores = []
            for j in range(i + 1):
                part = contract(mine, qkv_ref[j ^ s, :, lanes : 2 * lanes], 1, 1)
                if j == i:
                    part = jnp.where(column <= row, part, masked_score)
                scores.append(part)
            top = functools.reduce(jnp.maximum, scores)
            top = jnp.max(top, axis=-1, keepdims=True)
            total = None
            update = None
            for j in range(i + 1):
                weights = jnp.exp(scores[j] - top)
                term = jnp.dot(
                    weights.astype(low), qkv_ref[j ^ s, :, 2 * lanes :], preferred_element_type=full
                )
                update = term if update is None else update + term
                total = weights if total is None else total + weights
            total = jnp.sum(total, axis=-1, keepdims=True)
            joined = joined + head_lanes(update / total, head, pair, head_dim)
            lse = jnp.broadcast_to(top + jnp.log(total), (block, 128))
            lse_ref[here, head : head + 1, :] = jnp.transpose(lse)[0:1, :]
        exact_ref[here] = joined
        low_ref[here] = joined.astype(low)


def attend(place, qkv, pair, head_dim):
    count, seqs, block, columns = qkv.shape
    lanes = pair * head_dim
    groups = columns // (3 * lanes)
    spec = lambda width: pl.BlockSpec((count, None, block, width), lambda b, g, place: (0, b, 0, g))
    return pl.pallas_call(
        functools.partial(attend_kernel, pair, head_dim),
        grid_spec=pltpu.PrefetchScalarGridSpec(
            num_scalar_prefetch=1,
            grid=(seqs, groups),
            in_specs=[spec(3 * lanes)],
            out_specs=[
                spec(lanes),
                spec(lanes),
                pl.BlockSpec((count, None, None, pair, block), lambda b, g, place: (0, b, g, 0, 0)),
            ],
        ),
        out_shape=[
            jax.ShapeDtypeStruct((count, seqs, block, groups * lanes), full),
            jax.ShapeDtypeStruct((count, seqs, block, groups * lanes), low),
            jax.ShapeDtypeStruct((count, seqs, groups, pair, block), full),
        ],
        compiler_params=pltpu.CompilerParams(vmem_limit_bytes=kernel_memory),
        name="attend",
    )(place, qkv)


def attend_back_kernel(pair, head_dim, place, qkv_ref, exact_ref, grad_ref, lse_ref, cos_ref, sin_ref, out_ref, key_ref, value_ref):
    count, block, lanes3 = qkv_ref.shape
    lanes = lanes3 // 3
    scale = 1.0 / math.sqrt(head_dim)
    s = place[0]
    row = lax.broadcasted_iota(jnp.int32, (block, block), 0)
    column = lax.broadcasted_iota(jnp.int32, (block, block), 1)
    key_ref[...] = jnp.zeros_like(key_ref)
    value_ref[...] = jnp.zeros_like(value_ref)

    def back(total, at):
        kept = total.astype(low).astype(full)
        return turn(kept, cos_ref[at], -sin_ref[at], head_dim).astype(low)

    for i in range(count):
        here = i ^ s
        query = qkv_ref[here, :, 0:lanes] * jnp.asarray(scale, low)
        grad = grad_ref[here]
        product = exact_ref[here] * grad.astype(full)
        joined = jnp.zeros((block, lanes), full)
        for head in range(pair):
            mine = head_lanes(query, head, pair, head_dim)
            mine_grad = head_lanes(grad, head, pair, head_dim)
            delta = jnp.sum(
                jnp.transpose(head_lanes(product, head, pair, head_dim)), axis=0, keepdims=True
            )
            lse = lse_ref[here, head : head + 1, :]
            update = None
            for j in range(i + 1):
                there = j ^ s
                key = qkv_ref[there, :, lanes : 2 * lanes]
                value = qkv_ref[there, :, 2 * lanes :]
                scores = contract(key, mine, 1, 1)
                if j == i:
                    scores = jnp.where(row <= column, scores, masked_score)
                probs = jnp.exp(scores - lse)
                prob_grad = contract(value, mine_grad, 1, 1)
                score_grad = (probs * (prob_grad - delta)).astype(low)
                value_ref[j] += jnp.dot(probs.astype(low), mine_grad, preferred_element_type=full)
                key_ref[j] += jnp.dot(score_grad, mine, preferred_element_type=full)
                term = contract(score_grad, key, 0, 0)
                update = term if update is None else update + term
            joined = joined + head_lanes(update, head, pair, head_dim)
        out_ref[here, :, 0:lanes] = back(joined * scale, here)
    for j in range(count):
        there = j ^ s
        out_ref[there, :, lanes : 2 * lanes] = back(key_ref[j], there)
        out_ref[there, :, 2 * lanes :] = value_ref[j].astype(low)


def attend_back(place, qkv, exact, grad, lse, cosine, sine, pair, head_dim):
    count, seqs, block, columns = qkv.shape
    lanes = pair * head_dim
    groups = columns // (3 * lanes)
    spec = lambda width: pl.BlockSpec((count, None, block, width), lambda b, g, place: (0, b, 0, g))
    table = pl.BlockSpec((count, block, lanes), lambda b, g, place: (0, 0, 0))
    return pl.pallas_call(
        functools.partial(attend_back_kernel, pair, head_dim),
        grid_spec=pltpu.PrefetchScalarGridSpec(
            num_scalar_prefetch=1,
            grid=(seqs, groups),
            in_specs=[
                spec(3 * lanes),
                spec(lanes),
                spec(lanes),
                pl.BlockSpec((count, None, None, pair, block), lambda b, g, place: (0, b, g, 0, 0)),
                table,
                table,
            ],
            out_specs=spec(3 * lanes),
            scratch_shapes=[
                pltpu.VMEM((count, block, lanes), full),
                pltpu.VMEM((count, block, lanes), full),
            ],
        ),
        out_shape=jax.ShapeDtypeStruct(qkv.shape, low),
        compiler_params=pltpu.CompilerParams(vmem_limit_bytes=kernel_memory),
        name="attend_back",
    )(place, qkv, exact, grad, lse, cosine, sine)


def unproject_kernel(x_ref, mixed_ref, hidden_ref, in_ref, up_ref, norms_ref, out_ref, sums_ref):
    unit, _ = normalised(x_ref[...].astype(full))
    attn = contract(mixed_ref[...], in_ref[...], 1, 1)
    ff = contract(hidden_ref[...], up_ref[...], 1, 1)
    out_ref[...] = attn * norms_ref[0:1, :] + ff * norms_ref[2:3, :]
    sums = [attn * unit, attn, ff * unit, ff]
    sums = jnp.concatenate([jnp.sum(a, axis=0, keepdims=True) for a in sums], 0)

    @pl.when(pl.program_id(0) == 0)
    def _():
        sums_ref[...] = sums

    @pl.when(pl.program_id(0) > 0)
    def _():
        sums_ref[...] += sums


def unproject(x, mixed, hidden, in_weight, up_weight, norms, block):
    rows, width = x.shape
    whole = lambda i: (0, 0)
    step = lambda i: (i, 0)
    return pl.pallas_call(
        unproject_kernel,
        grid=(rows // block,),
        in_specs=[
            pl.BlockSpec((block, width), step),
            pl.BlockSpec((block, mixed.shape[1]), step),
            pl.BlockSpec((block, hidden.shape[1]), step),
            pl.BlockSpec(in_weight.shape, whole),
            pl.BlockSpec(up_weight.shape, whole),
            pl.BlockSpec((4, width), whole),
        ],
        out_specs=[pl.BlockSpec((block, width), step), pl.BlockSpec((4, width), whole)],
        out_shape=[
            jax.ShapeDtypeStruct((rows, width), full),
            jax.ShapeDtypeStruct((4, width), full),
        ],
        compiler_params=pltpu.CompilerParams(vmem_limit_bytes=kernel_memory),
        name="unproject",
    )(x, mixed, hidden, in_weight, up_weight, norms)


def on_device(
    tokens,
    input_weight,
    input_bias,
    output_weight,
    output_bias,
    up_weight,
    up_bias,
    down_weight,
    down_bias,
    attention_gain,
    attention_shift,
    feedforward_gain,
    feedforward_shift,
    cotangent,
):
    at = Layout()
    dp, seq, rank = at.dp, at.seq, at.rank
    seqs, block, width = tokens.shape
    shard = input_weight.shape[0]
    units = down_weight.shape[0]
    head_dim = width // HEADS
    heads = HEADS // seq
    pair = 2 if heads % 2 == 0 else 1
    groups = heads // pair
    lanes = pair * head_dim
    span = heads * head_dim
    place = rank.astype(jnp.int32).reshape(1)

    vectors = (input_bias, output_bias, up_bias, down_bias, attention_gain, attention_shift, feedforward_gain, feedforward_shift)
    sizes = [v.shape[0] for v in vectors]
    padded = -sum(sizes) % 128
    gathered = at.small_gather(jnp.concatenate(vectors + (jnp.zeros((padded,), low),)))
    edges = np.cumsum([0] + sizes)
    bias_in, bias_out, bias_up, bias_down, gain_attn, shift_attn, gain_ff, shift_ff = (
        gathered[:, :, edges[i] : edges[i + 1]].reshape(-1).astype(full) for i in range(8)
    )
    norms = jnp.stack([gain_attn, shift_attn, gain_ff, shift_ff], 0)

    in_split = input_weight.reshape(shard, 3, seq, groups, lanes)
    up_split = up_weight.reshape(shard, dp, seq, units)
    out_split = output_weight.reshape(shard, seq, span)

    def head_piece(spot):
        mixed = jnp.swapaxes(pick(in_split, spot, 2), 1, 2).reshape(shard, 3 * span)
        return jnp.concatenate([mixed, pick(out_split, spot, 1)], 1)

    def unit_piece(spot):
        return pick(up_split, spot, 2).reshape(shard, dp * units)

    tokens_all = at.seq_gather(tokens)
    head_rows = place_at(at.seq_exchange(head_piece), at.seq_spots(), 0)
    head_all = at.dp_gather(head_rows.reshape(seq * shard, 4 * span)).reshape(width, 4 * span)
    unit_rows = place_at(at.seq_exchange(unit_piece), at.seq_spots(), 0)
    up_all = at.dp_gather(unit_rows.reshape(seq * shard, dp * units)).reshape(width, dp * units)
    down_all = at.dp_gather(down_weight).reshape(dp * units, width)
    in_all = head_all[:, : 3 * span]
    out_split_all = head_all[:, 3 * span :].reshape(seq, span, span)
    out_all = place_at(
        at.seq_exchange(lambda spot: pick(out_split_all, spot, 0)), at.seq_spots(), 1
    ).reshape(span, width)
    cot_all = at.seq_gather(cotangent)

    rows = seq * seqs * block
    x = jnp.stack(tokens_all, 0).reshape(rows, width)
    cot = jnp.stack(cot_all, 0).reshape(rows, width)

    in_bias_mine = jnp.swapaxes(
        pick(bias_in.reshape(3, seq, groups, lanes), rank, 1), 0, 1
    ).reshape(1, 3 * span)
    up_bias_mine = pick(bias_up.reshape(dp, seq, units), rank, 1).reshape(dp * units)

    cos_table, sin_table = rotary_tables(seq * block, lanes, head_dim)
    normed_attn, normed_ff, qkv = project(
        place, x, in_all, in_bias_mine, norms, jnp.asarray(cos_table), jnp.asarray(sin_table),
        block, seqs, lanes, head_dim,
    )
    qkv = qkv.reshape(seq, seqs, block, 3 * span)
    exact, attended, lse = attend(place, qkv, pair, head_dim)
    attended = attended.reshape(rows, span)

    hidden = jnp.dot(normed_ff, up_all, preferred_element_type=full) + up_bias_mine
    tail = 0.5 * (1.0 + lax.erf(hidden * np.float32(math.sqrt(0.5))))
    bell = jnp.exp(-0.5 * hidden * hidden) * np.float32(1.0 / math.sqrt(2.0 * math.pi))
    active = (hidden * tail).astype(low)
    slope = (tail + hidden * bell).astype(low)

    out_part = jnp.dot(attended, out_all, preferred_element_type=full) + jnp.dot(
        active, down_all, preferred_element_type=full
    )
    out_part = out_part.reshape(seq, seqs, block, width)
    out_sum = at.seq_reduce([out_part[k] for k in range(seq)])
    output = (tokens.astype(full) + out_sum + (bias_out + bias_down)).astype(low)

    attended_grad = contract(cot, out_all, 1, 1).astype(low)
    hidden_grad = (contract(cot, down_all, 1, 1) * slope.astype(full)).astype(low)
    down_grad = contract(active, cot, 0, 0)
    out_grad = contract(attended, cot, 0, 0)
    up_grad = contract(normed_ff, hidden_grad, 0, 0)

    order = [rank ^ k for k in range(seq)]
    tables = [
        jnp.stack([pick(jnp.asarray(t.reshape(seq, block, lanes)), spot, 0) for spot in order], 0)
        for t in (cos_table, sin_table)
    ]
    mixed_grad = attend_back(
        place, qkv, exact, attended_grad.reshape(seq, seqs, block, span), lse, *tables, pair, head_dim
    ).reshape(rows, 3 * span)
    in_grad = contract(normed_attn, mixed_grad, 0, 0)
    unit_grad, norm_sums = unproject(x, mixed_grad, hidden_grad, in_all, up_all, norms, block)
    unit_grad = unit_grad.reshape(seq, seqs, block, width)
    unit_sum = at.seq_reduce([unit_grad[k] for k in range(seq)])
    unit, rstd = normalised(tokens.astype(full))
    token_grad = cotangent.astype(full) + rstd * (
        unit_sum
        - jnp.mean(unit_sum, axis=-1, keepdims=True)
        - unit * jnp.mean(unit_sum * unit, axis=-1, keepdims=True)
    )
    token_grad = token_grad.astype(low)

    down_sum = at.dp_reduce(down_grad.reshape(dp, units, width))
    out_pieces = out_grad.astype(low).reshape(span, seq, span)
    out_grad = place_at(
        at.seq_exchange(lambda spot: pick(out_pieces, spot, 1)), at.seq_spots(), 0
    )
    out_sum_rows = at.dp_reduce(out_grad.reshape(dp, seq * shard, span))
    up_sum = at.dp_reduce(up_grad.reshape(dp, seq * shard, dp * units))
    in_sum = at.dp_reduce(in_grad.reshape(dp, seq * shard, 3 * span))

    def hand_back(total):
        split = total.reshape(seq, shard, total.shape[1]).astype(low)
        return [p.astype(full) for p in at.seq_exchange(lambda spot: pick(split, spot, 0))]

    up_final = place_at(
        [p.reshape(shard, dp, units) for p in hand_back(up_sum)], at.seq_spots(), 2
    ).reshape(shard, dp * seq * units)
    out_final = place_at(hand_back(out_sum_rows), at.seq_spots(), 1).reshape(shard, width)
    in_final = place_at(
        [
            jnp.swapaxes(p.reshape(shard, groups, 3, lanes), 1, 2).reshape(shard, 3, span)
            for p in hand_back(in_sum)
        ],
        at.seq_spots(),
        2,
    ).reshape(shard, 3 * width)

    in_bias_sum = jnp.sum(mixed_grad.astype(full), axis=0).reshape(groups, 3, lanes)
    in_bias_sum = jnp.swapaxes(in_bias_sum, 0, 1).reshape(3, 1, span)
    in_bias_sum = lax.dynamic_update_slice_in_dim(jnp.zeros((3, seq, span), full), in_bias_sum, rank, 1)
    up_bias_sum = jnp.sum(hidden_grad.astype(full), axis=0).reshape(dp, 1, units)
    up_bias_sum = lax.dynamic_update_slice_in_dim(jnp.zeros((dp, seq, units), full), up_bias_sum, rank, 1)
    out_bias_sum = jnp.sum(cotangent.astype(full), axis=(0, 1))
    in_bias_sum = in_bias_sum.reshape(3 * width)
    small = [
        in_bias_sum[: 2 * width],
        in_bias_sum[2 * width :],
        out_bias_sum,
        up_bias_sum,
        norm_sums[0],
        norm_sums[1],
        norm_sums[2],
        norm_sums[3],
    ]
    small = [v.reshape(dp, seq, -1) for v in small]
    edges = np.cumsum([0] + [v.shape[2] for v in small])
    total = at.small_reduce(jnp.concatenate(small, 2))
    (query_key_bias, value_bias, out_bias, up_bias_grad, *norm_grads) = [
        total[edges[i] : edges[i + 1]] for i in range(8)
    ]
    return (
        output,
        token_grad,
        in_final,
        query_key_bias,
        value_bias,
        out_final,
        out_bias,
        up_final,
        up_bias_grad,
        down_sum,
        out_bias,
        *norm_grads,
    )


def solution(mesh):
    rows = P(("dp", "seq"), None)
    flat = P(("dp", "seq"))
    held = P("dp", "seq", None)
    return jax.shard_map(
        on_device,
        mesh=mesh,
        in_specs=(held, rows, flat, rows, flat, rows, flat, rows, flat, flat, flat, flat, flat, held),
        out_specs=(held, held, rows, flat, flat, rows, flat, rows, flat, rows, flat, flat, flat, flat, flat),
        check_vma=False,
    )
```

```python
import functools
import math

import jax
import jax.numpy as jnp
import numpy as np
from jax import lax
from jax.experimental import pallas as pl
from jax.experimental.pallas import tpu as pltpu
from jax.sharding import PartitionSpec as P

HEADS = 16
ROT = 16

norm_eps = 1e-05
masked_score = -1e30
low = jnp.bfloat16
full = jnp.float32
kernel_memory = 56 * 1024 * 1024


def place_at(pieces, spots, axis):
    count = len(pieces)
    shape = list(pieces[0].shape)
    shape.insert(axis, count)
    held = jnp.zeros(shape, pieces[0].dtype)
    for piece, spot in zip(pieces, spots):
        held = lax.dynamic_update_index_in_dim(held, piece, spot, axis)
    return held


def pick(array, spot, axis):
    return lax.dynamic_index_in_dim(array, spot, axis, keepdims=False)


def effort(micros):
    return pl.CostEstimate(flops=int(micros * 1.1e9), bytes_accessed=1, transcendentals=0)


anywhere = pl.BlockSpec(memory_space=pl.ANY)


def pass_kernel(*refs):
    del refs


def after(array, *others):
    return pl.pallas_call(
        pass_kernel,
        in_specs=[anywhere] * (1 + len(others)),
        out_specs=anywhere,
        out_shape=jax.ShapeDtypeStruct(array.shape, array.dtype),
        input_output_aliases={0: 0},
        name="after",
    )(array, *others)


def chosen_units(ref, rank, ranks, units):
    runs = ref.shape[1] // (ranks * units)
    parts = []
    for run in range(runs):
        first = run * ranks * units
        if units % 128 == 0:
            parts.append(ref[:, pl.ds(pl.multiple_of(first + rank * units, 128), units)])
        else:
            whole = ref[:, first : first + ranks * units]
            part = jnp.zeros((ref.shape[0], units), ref.dtype)
            for r in range(ranks):
                part = jnp.where(rank == r, whole[:, r * units : (r + 1) * units], part)
            parts.append(part)
    return jnp.concatenate(parts, 1)


def deal_kernel(ranks, groups, vectors, units, place, in_ref, out_ref, up_ref, *refs):
    shard, width = out_ref.shape
    span = width // ranks
    lanes = span // groups
    wide = 4 * span
    slot = wide // vectors
    row = jnp.concatenate(
        [
            r[...] if r.shape[1] == slot else jnp.concatenate([r[...], jnp.zeros((1, slot - r.shape[1]), low)], 1)
            for r in refs[:vectors]
        ],
        1,
    )
    rows = jnp.concatenate([row, jnp.zeros((15, wide), low)], 0)
    for k in range(ranks):
        rank = place[0] ^ k
        dealt = refs[vectors + k]

        def columns(ref, start):
            first = start + rank * span
            if span % 128 == 0:
                return ref[:, pl.ds(pl.multiple_of(first, 128), span)]
            whole = ref[:, start : start + width]
            chosen = jnp.zeros((shard, span), low)
            for r in range(ranks):
                chosen = jnp.where(rank == r, whole[:, r * span : (r + 1) * span], chosen)
            return chosen

        for kind in range(3):
            mine = columns(in_ref, kind * width)
            for group in range(groups):
                target = (group * 3 + kind) * lanes
                dealt[:shard, target : target + lanes] = mine[:, group * lanes : (group + 1) * lanes]
        dealt[:shard, 3 * span :] = columns(out_ref, 0)
        dealt[shard : shard + 16, :] = rows
        dealt[shard + 16 :, :] = chosen_units(up_ref, rank, ranks, units)


def deal(place, input_weight, output_weight, up_weight, vectors, ranks, groups, units):
    shard, width = output_weight.shape
    arrays = [input_weight, output_weight, up_weight] + [v[None] for v in vectors]
    shape = (2 * shard + 16, 4 * width // ranks)
    vmem = pl.BlockSpec(memory_space=pltpu.VMEM)
    return pl.pallas_call(
        functools.partial(deal_kernel, ranks, groups, len(vectors), units),
        in_specs=[pl.BlockSpec(memory_space=pltpu.SMEM)] + [vmem] * len(arrays),
        out_specs=[vmem] * ranks,
        out_shape=[jax.ShapeDtypeStruct(shape, low)] * ranks,
        compiler_params=pltpu.CompilerParams(vmem_limit_bytes=kernel_memory),
        name="deal",
    )(place, *arrays)


def gather_heads_kernel(count, shard, place, *refs):
    out, units = refs[count:]
    for k in range(count):
        rank = place[0] ^ k
        if shard % 16 == 0:
            here = pl.ds(pl.multiple_of(rank * shard, 16), shard)
            out[here, :] = refs[k][:shard, :]
            units[here, :] = refs[k][shard + 16 :, :]
        else:
            for r in range(count):

                @pl.when(rank == r)
                def _(r=r, k=k):
                    out[r * shard : (r + 1) * shard, :] = refs[k][:shard, :]
                    units[r * shard : (r + 1) * shard, :] = refs[k][shard + 16 :, :]

    row = lax.broadcasted_iota(jnp.int32, (out.shape[0] - count * shard, 1), 0)
    vectors = jnp.zeros((out.shape[0] - count * shard, out.shape[1]), full)
    for k in range(count):
        mine = refs[k][shard : shard + 1, :].astype(full)
        vectors = jnp.where(row == (place[0] ^ k), mine, vectors)
    out[count * shard :, :] = vectors.astype(low)


def gather_heads(place, pieces, shard):
    count = len(pieces)
    wide = pieces[0].shape[1]
    vmem = pl.BlockSpec(memory_space=pltpu.VMEM)
    return pl.pallas_call(
        functools.partial(gather_heads_kernel, count, shard),
        in_specs=[pl.BlockSpec(memory_space=pltpu.SMEM)] + [vmem] * count,
        out_specs=[vmem, vmem],
        out_shape=[
            jax.ShapeDtypeStruct((count * shard + count + -count % 16, wide), low),
            jax.ShapeDtypeStruct((count * shard, wide), low),
        ],
        compiler_params=pltpu.CompilerParams(vmem_limit_bytes=kernel_memory),
        name="gather_heads",
    )(place, *pieces)


def cut_kernel(x_ref, y_ref, *refs):
    first, second = refs[-2:]
    first[...] = x_ref[...]
    second[...] = y_ref[...]


def cut(x, y, wait):
    seqs, block, width = x.shape
    half = (seqs, block // 2, width)
    return pl.pallas_call(
        cut_kernel,
        grid=(1,),
        in_specs=[pl.BlockSpec(half, lambda i: (0, 0, 0)), pl.BlockSpec(half, lambda i: (0, 1, 0))]
        + [anywhere] * len(wait),
        out_specs=[pl.BlockSpec(half, lambda i: (0, 0, 0))] * 2,
        out_shape=[jax.ShapeDtypeStruct(half, x.dtype)] * 2,
        compiler_params=pltpu.CompilerParams(vmem_limit_bytes=kernel_memory),
        name="cut",
    )(x, y, *wait)


def lay_columns_kernel(count, place, *refs):
    out = refs[count]
    span = refs[0].shape[1]
    for k in range(count):
        rank = place[0] ^ k
        if span % 128 == 0:
            out[:, pl.ds(pl.multiple_of(rank * span, 128), span)] = refs[k][...]
        else:
            for r in range(count):

                @pl.when(rank == r)
                def _(r=r, k=k):
                    out[:, r * span : (r + 1) * span] = refs[k][...]


def lay_columns(place, pieces):
    count = len(pieces)
    rows, span = pieces[0].shape
    vmem = pl.BlockSpec(memory_space=pltpu.VMEM)
    return pl.pallas_call(
        functools.partial(lay_columns_kernel, count),
        in_specs=[pl.BlockSpec(memory_space=pltpu.SMEM)] + [vmem] * count,
        out_specs=vmem,
        out_shape=jax.ShapeDtypeStruct((rows, count * span), pieces[0].dtype),
        compiler_params=pltpu.CompilerParams(vmem_limit_bytes=kernel_memory),
        name="lay_columns",
    )(place, *pieces)


def lay_kernel(count, place, *refs):
    out = refs[count]
    for k in range(count):
        out[place[0] ^ k] = refs[k][...]


def lay(place, pieces):
    count = len(pieces)
    shape = (count,) + pieces[0].shape
    return pl.pallas_call(
        functools.partial(lay_kernel, count),
        grid_spec=pltpu.PrefetchScalarGridSpec(
            num_scalar_prefetch=1,
            grid=(1,),
            in_specs=[pl.BlockSpec(p.shape, lambda i, place, n=p.ndim: (0,) * n) for p in pieces],
            out_specs=pl.BlockSpec(shape, lambda i, place: (0,) * len(shape)),
        ),
        out_shape=jax.ShapeDtypeStruct(shape, pieces[0].dtype),
        compiler_params=pltpu.CompilerParams(vmem_limit_bytes=kernel_memory),
        name="lay",
    )(place, *pieces)


class Layout:
    def __init__(self):
        self.dp = lax.axis_size("dp")
        self.seq = lax.axis_size("seq")
        self.rank = lax.axis_index("seq")

    def seq_swap(self, array, k):
        return lax.ppermute(array, "seq", [(i, i ^ k) for i in range(self.seq)])

    def seq_exchange(self, piece_for):
        return [piece_for(self.rank)] + [
            self.seq_swap(piece_for(self.rank ^ k), k) for k in range(1, self.seq)
        ]

    def seq_trade(self, array, place):
        return lay(place, self.seq_exchange(lambda spot: pick(array, spot, 0)))

    def seq_spots(self):
        return [self.rank ^ k for k in range(self.seq)]

    def seq_gather_direct(self, array):
        return [array] + [self.seq_swap(array, k) for k in range(1, self.seq)]

    def seq_gather(self, array):
        if self.seq != 4:
            return self.seq_gather_direct(array)
        return self.seq_gather_far(self.seq_gather_near(array))

    def seq_gather_near(self, array):
        if self.seq != 4:
            return self.seq_gather_direct(array)
        return [array, self.seq_swap(array, 1), self.seq_swap(array, 2)]

    def seq_gather_far(self, near, *wait):
        if self.seq != 4:
            return near
        first, second = cut(near[1], near[2], wait)
        return near + [self.seq_swap(first, 2), self.seq_swap(second, 1)]

    def seq_reduce_far(self, part):
        half = part.shape[1] // 2
        return self.seq_swap(part[:, half:], 2), self.seq_swap(part[:, :half], 1)

    def seq_reduce_near(self, parts, far):
        half = parts[0].shape[1] // 2
        for_x, for_y = (a.astype(full) for a in far)
        p1, p2 = parts
        p1 = jnp.concatenate([p1[:, :half], (p1[:, half:].astype(full) + for_x).astype(low)], 1)
        p2 = jnp.concatenate([(p2[:, :half].astype(full) + for_y).astype(low), p2[:, half:]], 1)
        return self.seq_swap(p1, 1), self.seq_swap(p2, 2)

    def seq_turnover(self, array):
        return lax.all_to_all(array, "seq", 0, 0, tiled=True)

    def z_turn(self, array, k):
        return lax.ppermute(array, "dp", [(i, (i + k) % self.dp) for i in range(self.dp)])

    def small_reduce(self, array):
        array = sum(self.seq_exchange(lambda spot: pick(array, spot, 1)))
        cores = 2 if self.dp % 2 == 0 else 1
        here = lax.axis_index("dp")
        core, z = here % cores, here // cores
        line = self.dp // cores
        pairs = array.reshape((line, cores) + array.shape[1:])
        if cores == 2:
            swap = [(i, i ^ 1) for i in range(self.dp)]
            array = pick(pairs, core, 1) + lax.ppermute(pick(pairs, 1 - core, 1), "dp", swap)
        else:
            array = pairs[:, 0]
        total = pick(array, z, 0)
        for k in range(1, line):
            total = total + self.z_turn(pick(array, (z + k) % line, 0), k * cores)
        return total

    def dp_gather(self, array):
        return lax.all_gather(array, "dp", axis=0, tiled=False)

    def dp_reduce(self, array):
        return lax.psum_scatter(array, "dp", scatter_dimension=0, tiled=False)


def rotary_tables(length, lanes, head_dim):
    half = ROT // 2
    exponent = -np.arange(0, ROT, 2, dtype=np.float32) / np.float32(ROT)
    frequency = np.float32(10000.0) ** exponent
    phase = np.arange(length, dtype=np.float32)[:, None] * frequency[None, :]
    cosine = np.ones((length, head_dim), np.float32)
    sine = np.zeros((length, head_dim), np.float32)
    cosine[:, :half] = cosine[:, half:ROT] = np.cos(phase)
    sine[:, :half] = -np.sin(phase)
    sine[:, half:ROT] = np.sin(phase)
    copies = lanes // head_dim
    return np.tile(cosine, (1, copies)), np.tile(sine, (1, copies))


def roll_lanes(x, shift):
    size = x.shape[-1]
    if size % 128 == 0:
        return pltpu.roll(x, shift % size, x.ndim - 1)
    return jnp.roll(x, shift, -1)


def turn(x, cosine, sine, head_dim):
    half = ROT // 2
    lane = lax.broadcasted_iota(jnp.int32, x.shape, 1) % head_dim
    swapped = jnp.where(lane < half, roll_lanes(x, -half), roll_lanes(x, half))
    return x * cosine + swapped * sine


def normalised(x):
    mean = jnp.mean(x, axis=-1, keepdims=True)
    centered = x - mean
    variance = jnp.mean(centered * centered, axis=-1, keepdims=True)
    rstd = lax.rsqrt(variance + norm_eps)
    return centered * rstd, rstd


def project_kernel(head_dim, lanes, shard, columns, stacked, place, head_ref, bias_ref, norms_ref, cos_ref, sin_ref, *refs):
    pieces, (x_out, attn_ref, ff_ref, qkv_ref) = refs[:-4], refs[-4:]
    block, width = x_out.shape
    if stacked:
        x_out[...] = pieces[0][...]
    else:
        step = pl.program_id(0)
        first = 0
        for piece in pieces:
            rows = piece.shape[0]
            inside = first % block

            @pl.when(step == first // block)
            def _(piece=piece, inside=inside, rows=rows):
                x_out[inside : inside + rows, :] = piece[...]

            first += rows
    unit, _ = normalised(x_out[...].astype(full))
    normed = (unit * norms_ref[0:1, :] + norms_ref[1:2, :]).astype(low)
    attn_ref[...] = normed
    ff_ref[...] = (unit * norms_ref[2:3, :] + norms_ref[3:4, :]).astype(low)
    weight = head_ref[:, :shard, :columns].reshape(width, columns)
    mixed = jnp.dot(normed, weight, preferred_element_type=full) + bias_ref[...]
    cosine, sine = cos_ref[...], sin_ref[...]
    for group in range(columns // lanes):
        span = slice(group * lanes, (group + 1) * lanes)
        part = mixed[:, span]
        if group % 3 < 2:
            part = turn(part, cosine, sine, head_dim)
        qkv_ref[:, span] = part.astype(low)


def project(place, pieces, head, bias, norms, cosine, sine, block, seqs, lanes, head_dim, shard):
    stacked = len(pieces) == 1
    width = pieces[0].shape[1]
    rows = sum(p.shape[0] for p in pieces)
    columns = bias.shape[1]
    whole = lambda i, place: (0, 0)
    step = lambda i, place: (i, 0)
    spot = lambda i, place: ((i // seqs) ^ place[0], 0)
    if stacked:
        piece_specs = [pl.BlockSpec((block, width), step)]
    else:
        piece_specs = [pl.BlockSpec(p.shape, whole) for p in pieces]
    return pl.pallas_call(
        functools.partial(project_kernel, head_dim, lanes, shard, columns, stacked),
        grid_spec=pltpu.PrefetchScalarGridSpec(
            num_scalar_prefetch=1,
            grid=(rows // block,),
            in_specs=[
                pl.BlockSpec(head.shape, lambda i, place: (0, 0, 0)),
                pl.BlockSpec((1, columns), whole),
                pl.BlockSpec((4, width), whole),
                pl.BlockSpec((block, lanes), spot),
                pl.BlockSpec((block, lanes), spot),
            ]
            + piece_specs,
            out_specs=[
                pl.BlockSpec((block, width), step),
                pl.BlockSpec((block, width), step),
                pl.BlockSpec((block, width), step),
                pl.BlockSpec((block, columns), step),
            ],
        ),
        out_shape=[
            jax.ShapeDtypeStruct((rows, width), low),
            jax.ShapeDtypeStruct((rows, width), low),
            jax.ShapeDtypeStruct((rows, width), low),
            jax.ShapeDtypeStruct((rows, columns), low),
        ],
        compiler_params=pltpu.CompilerParams(vmem_limit_bytes=kernel_memory),
        cost_estimate=effort(12 * rows / 2048),
        name="project",
    )(place, head, bias, norms, cosine, sine, *pieces)


def contract(a, b, da, db):
    return lax.dot_general(a, b, (((da,), (db,)), ((), ())), preferred_element_type=full)


def head_lanes(x, head, pair, head_dim):
    if pair == 1:
        return x
    lane = lax.broadcasted_iota(jnp.int32, x.shape, 1)
    inside = (lane >= head * head_dim) & (lane < (head + 1) * head_dim)
    return jnp.where(inside, x, jnp.zeros_like(x))


def attend_kernel(pair, head_dim, place, qkv_ref, exact_ref, low_ref, lse_ref):
    count, block, lanes3 = qkv_ref.shape
    lanes = lanes3 // 3
    scale = 1.0 / math.sqrt(head_dim)
    s = place[0]
    row = lax.broadcasted_iota(jnp.int32, (block, block), 0)
    column = lax.broadcasted_iota(jnp.int32, (block, block), 1)
    for i in range(count):
        here = i ^ s
        query = qkv_ref[here, :, 0:lanes] * jnp.asarray(scale, low)
        joined = jnp.zeros((block, lanes), full)
        for head in range(pair):
            mine = head_lanes(query, head, pair, head_dim)
            scores = []
            for j in range(i + 1):
                part = contract(mine, qkv_ref[j ^ s, :, lanes : 2 * lanes], 1, 1)
                if j == i:
                    part = jnp.where(column <= row, part, masked_score)
                scores.append(part)
            top = functools.reduce(jnp.maximum, scores)
            top = jnp.max(top, axis=-1, keepdims=True)
            total = None
            update = None
            for j in range(i + 1):
                weights = jnp.exp(scores[j] - top)
                term = jnp.dot(
                    weights.astype(low), qkv_ref[j ^ s, :, 2 * lanes :], preferred_element_type=full
                )
                update = term if update is None else update + term
                total = weights if total is None else total + weights
            total = jnp.sum(total, axis=-1, keepdims=True)
            joined = joined + head_lanes(update / total, head, pair, head_dim)
            lse = jnp.broadcast_to(top + jnp.log(total), (block, 128))
            lse_ref[here, head : head + 1, :] = jnp.transpose(lse)[0:1, :]
        exact_ref[here] = joined
        low_ref[here] = joined.astype(low)


def attend(place, qkv, pair, head_dim):
    count, seqs, block, columns = qkv.shape
    lanes = pair * head_dim
    groups = columns // (3 * lanes)
    spec = lambda width: pl.BlockSpec((count, None, block, width), lambda b, g, place: (0, b, 0, g))
    return pl.pallas_call(
        functools.partial(attend_kernel, pair, head_dim),
        grid_spec=pltpu.PrefetchScalarGridSpec(
            num_scalar_prefetch=1,
            grid=(seqs, groups),
            in_specs=[spec(3 * lanes)],
            out_specs=[
                spec(lanes),
                spec(lanes),
                pl.BlockSpec((count, None, None, pair, block), lambda b, g, place: (0, b, g, 0, 0)),
            ],
        ),
        out_shape=[
            jax.ShapeDtypeStruct((count, seqs, block, groups * lanes), full),
            jax.ShapeDtypeStruct((count, seqs, block, groups * lanes), low),
            jax.ShapeDtypeStruct((count, seqs, groups, pair, block), full),
        ],
        compiler_params=pltpu.CompilerParams(vmem_limit_bytes=kernel_memory),
        cost_estimate=effort(18 * seqs * groups / 2),
        name="attend",
    )(place, qkv)


def attend_back_kernel(pair, head_dim, place, qkv_ref, exact_ref, grad_ref, lse_ref, cos_ref, sin_ref, *refs):
    out_ref, sum_ref, key_ref, value_ref = refs[-4:]
    count, block, lanes3 = qkv_ref.shape
    lanes = lanes3 // 3
    scale = 1.0 / math.sqrt(head_dim)
    s = place[0]
    row = lax.broadcasted_iota(jnp.int32, (block, block), 0)
    column = lax.broadcasted_iota(jnp.int32, (block, block), 1)
    key_ref[...] = jnp.zeros_like(key_ref)
    value_ref[...] = jnp.zeros_like(value_ref)
    query_sum = jnp.zeros((1, lanes), full)

    def back(total, at):
        kept = total.astype(low).astype(full)
        return turn(kept, cos_ref[at], -sin_ref[at], head_dim).astype(low)

    for i in range(count):
        here = i ^ s
        query = qkv_ref[here, :, 0:lanes] * jnp.asarray(scale, low)
        grad = grad_ref[here]
        product = exact_ref[here] * grad.astype(full)
        joined = jnp.zeros((block, lanes), full)
        for head in range(pair):
            mine = head_lanes(query, head, pair, head_dim)
            mine_grad = head_lanes(grad, head, pair, head_dim)
            delta = jnp.sum(
                jnp.transpose(head_lanes(product, head, pair, head_dim)), axis=0, keepdims=True
            )
            lse = lse_ref[here, head : head + 1, :]
            update = None
            for j in range(i + 1):
                there = j ^ s
                key = qkv_ref[there, :, lanes : 2 * lanes]
                value = qkv_ref[there, :, 2 * lanes :]
                scores = contract(key, mine, 1, 1)
                if j == i:
                    scores = jnp.where(row <= column, scores, masked_score)
                probs = jnp.exp(scores - lse)
                prob_grad = contract(value, mine_grad, 1, 1)
                score_grad = (probs * (prob_grad - delta)).astype(low)
                value_ref[j] += jnp.dot(probs.astype(low), mine_grad, preferred_element_type=full)
                key_ref[j] += jnp.dot(score_grad, mine, preferred_element_type=full)
                term = contract(score_grad, key, 0, 0)
                update = term if update is None else update + term
            joined = joined + head_lanes(update, head, pair, head_dim)
        final = back(joined * scale, here)
        out_ref[here, :, 0:lanes] = final
        query_sum = query_sum + jnp.sum(final.astype(full), axis=0, keepdims=True)
    key_sum = value_sum = jnp.zeros((1, lanes), full)
    for j in range(count):
        there = j ^ s
        final = back(key_ref[j], there)
        out_ref[there, :, lanes : 2 * lanes] = final
        key_sum = key_sum + jnp.sum(final.astype(full), axis=0, keepdims=True)
        final = value_ref[j].astype(low)
        out_ref[there, :, 2 * lanes :] = final
        value_sum = value_sum + jnp.sum(final.astype(full), axis=0, keepdims=True)
    sum_ref[0:1, :] = query_sum
    sum_ref[1:2, :] = key_sum
    sum_ref[2:3, :] = value_sum


def attend_back(place, qkv, exact, grad, lse, cosine, sine, pair, head_dim, wait):
    count, seqs, block, columns = qkv.shape
    lanes = pair * head_dim
    groups = columns // (3 * lanes)
    spec = lambda width: pl.BlockSpec((count, None, block, width), lambda b, g, place: (0, b, 0, g))
    table = pl.BlockSpec((count, block, lanes), lambda b, g, place: (0, 0, 0))
    return pl.pallas_call(
        functools.partial(attend_back_kernel, pair, head_dim),
        grid_spec=pltpu.PrefetchScalarGridSpec(
            num_scalar_prefetch=1,
            grid=(seqs, groups),
            in_specs=[
                spec(3 * lanes),
                spec(lanes),
                spec(lanes),
                pl.BlockSpec((count, None, None, pair, block), lambda b, g, place: (0, b, g, 0, 0)),
                table,
                table,
            ]
            + [anywhere] * len(wait),
            out_specs=[
                spec(3 * lanes),
                pl.BlockSpec((None, None, 3, lanes), lambda b, g, place: (b, g, 0, 0)),
            ],
            scratch_shapes=[
                pltpu.VMEM((count, block, lanes), full),
                pltpu.VMEM((count, block, lanes), full),
            ],
        ),
        out_shape=[
            jax.ShapeDtypeStruct(qkv.shape, low),
            jax.ShapeDtypeStruct((seqs, groups, 3, lanes), full),
        ],
        compiler_params=pltpu.CompilerParams(vmem_limit_bytes=kernel_memory),
        cost_estimate=effort(33 * seqs * groups / 2),
        name="attend_back",
    )(place, qkv, exact, grad, lse, cosine, sine, *wait)


def expand_kernel(x_ref, weight_ref, bias_ref, *refs):
    active_ref, slope_ref = refs[-2:]
    hidden = jnp.dot(x_ref[...], weight_ref[...], preferred_element_type=full) + bias_ref[...]
    tail = 0.5 * (1.0 + lax.erf(hidden * np.float32(math.sqrt(0.5))))
    bell = jnp.exp(-0.5 * hidden * hidden) * np.float32(1.0 / math.sqrt(2.0 * math.pi))
    active_ref[...] = (hidden * tail).astype(low)
    slope_ref[...] = (tail + hidden * bell).astype(low)


def expand(x, weight, bias, block, wait):
    rows, width = x.shape
    columns = weight.shape[1]
    whole = lambda i: (0, 0)
    step = lambda i: (i, 0)
    return pl.pallas_call(
        expand_kernel,
        grid=(rows // block,),
        in_specs=[
            pl.BlockSpec((block, width), step),
            pl.BlockSpec((width, columns), whole),
            pl.BlockSpec((1, columns), whole),
        ]
        + [anywhere] * len(wait),
        out_specs=[pl.BlockSpec((block, columns), step), pl.BlockSpec((block, columns), step)],
        out_shape=[jax.ShapeDtypeStruct((rows, columns), low)] * 2,
        compiler_params=pltpu.CompilerParams(vmem_limit_bytes=kernel_memory),
        cost_estimate=effort(12 * rows / 2048),
        name="expand",
    )(x, weight, bias, *wait)


def turnabout_kernel(stacked, attended_ref, active_ref, slope_ref, out_ref, down_ref, *refs):
    pieces, (cot_ref, part_ref, attended_grad_ref, hidden_grad_ref, sum_ref) = refs[:-5], refs[-5:]
    block = cot_ref.shape[0]
    step = pl.program_id(0)
    if stacked:
        cot_ref[...] = pieces[0][...]
    else:
        first = 0
        for piece in pieces:
            rows = piece.shape[0]
            inside = first % block

            @pl.when(step == first // block)
            def _(piece=piece, inside=inside, rows=rows):
                cot_ref[inside : inside + rows, :] = piece[...]

            first += rows
    part = jnp.dot(attended_ref[...], out_ref[...], preferred_element_type=full)
    part = part + jnp.dot(active_ref[...], down_ref[...], preferred_element_type=full)
    part_ref[...] = part.astype(low)
    cot = cot_ref[...]
    attended_grad_ref[...] = contract(cot, out_ref[...], 1, 1).astype(low)
    hidden = (contract(cot, down_ref[...], 1, 1) * slope_ref[...].astype(full)).astype(low)
    hidden_grad_ref[...] = hidden
    total = jnp.sum(hidden.astype(full), axis=0, keepdims=True)

    @pl.when(step == 0)
    def _():
        sum_ref[...] = total

    @pl.when(step > 0)
    def _():
        sum_ref[...] += total


def turnabout(attended, active, slope, out_weight, down_weight, pieces, block):
    stacked = len(pieces) == 1
    rows, span = attended.shape
    columns, width = down_weight.shape
    whole = lambda i: (0, 0)
    step = lambda i: (i, 0)
    if stacked:
        piece_specs = [pl.BlockSpec((block, width), step)]
    else:
        piece_specs = [pl.BlockSpec(p.shape, whole) for p in pieces]
    return pl.pallas_call(
        functools.partial(turnabout_kernel, stacked),
        grid=(rows // block,),
        in_specs=[
            pl.BlockSpec((block, span), step),
            pl.BlockSpec((block, columns), step),
            pl.BlockSpec((block, columns), step),
            pl.BlockSpec((span, width), whole),
            pl.BlockSpec((columns, width), whole),
        ]
        + piece_specs,
        out_specs=[
            pl.BlockSpec((block, width), step),
            pl.BlockSpec((block, width), step),
            pl.BlockSpec((block, span), step),
            pl.BlockSpec((block, columns), step),
            pl.BlockSpec((1, columns), whole),
        ],
        out_shape=[
            jax.ShapeDtypeStruct((rows, width), low),
            jax.ShapeDtypeStruct((rows, width), low),
            jax.ShapeDtypeStruct((rows, span), low),
            jax.ShapeDtypeStruct((rows, columns), low),
            jax.ShapeDtypeStruct((1, columns), full),
        ],
        compiler_params=pltpu.CompilerParams(vmem_limit_bytes=kernel_memory),
        cost_estimate=effort(14 * rows / 2048),
        name="turnabout",
    )(attended, active, slope, out_weight, down_weight, *pieces)


def unproject_kernel(x_ref, mixed_ref, hidden_ref, in_ref, up_ref, norms_ref, *refs):
    out_ref, sums_ref = refs[-2:]
    unit, _ = normalised(x_ref[...].astype(full))
    width, columns = x_ref.shape[1], mixed_ref.shape[1]
    in_weight = in_ref[:, : width // in_ref.shape[0], :columns].reshape(width, columns)
    attn = contract(mixed_ref[...], in_weight, 1, 1)
    ff = contract(hidden_ref[...], up_ref[...], 1, 1)
    out_ref[...] = (attn * norms_ref[0:1, :] + ff * norms_ref[2:3, :]).astype(low)
    sums = [attn * unit, attn, ff * unit, ff]
    sums = jnp.concatenate([jnp.sum(a, axis=0, keepdims=True) for a in sums], 0)

    @pl.when(pl.program_id(0) == 0)
    def _():
        sums_ref[...] = sums

    @pl.when(pl.program_id(0) > 0)
    def _():
        sums_ref[...] += sums


def unproject(x, mixed, hidden, in_weight, up_weight, norms, block, first, count, wait):
    rows, width = count * block, x.shape[1]
    whole = lambda i: (0, 0)
    step = lambda i: (i + first, 0)
    here = lambda i: (i, 0)
    return pl.pallas_call(
        unproject_kernel,
        grid=(rows // block,),
        in_specs=[
            pl.BlockSpec((block, width), step),
            pl.BlockSpec((block, mixed.shape[1]), step),
            pl.BlockSpec((block, hidden.shape[1]), step),
            pl.BlockSpec(in_weight.shape, lambda i: (0, 0, 0)),
            pl.BlockSpec(up_weight.shape, whole),
            pl.BlockSpec((4, width), whole),
        ]
        + [anywhere] * len(wait),
        out_specs=[pl.BlockSpec((block, width), here), pl.BlockSpec((4, width), whole)],
        out_shape=[
            jax.ShapeDtypeStruct((rows, width), low),
            jax.ShapeDtypeStruct((4, width), full),
        ],
        compiler_params=pltpu.CompilerParams(vmem_limit_bytes=kernel_memory),
        cost_estimate=effort(18 * rows / 2048),
        name="unproject",
    )(x, mixed, hidden, in_weight, up_weight, norms, *wait)


def reduce_steps(at, far, near):
    if at.seq != 4:
        got = [at.seq_swap(a, k + 1) for k, a in enumerate(near())]
        return [], got + [at.seq_swap(far, at.seq - 1)]
    first = at.seq_reduce_far(far)
    return first, list(at.seq_reduce_near(near(), first))


def on_device(
    tokens,
    input_weight,
    input_bias,
    output_weight,
    output_bias,
    up_weight,
    up_bias,
    down_weight,
    down_bias,
    attention_gain,
    attention_shift,
    feedforward_gain,
    feedforward_shift,
    cotangent,
):
    at = Layout()
    dp, seq, rank = at.dp, at.seq, at.rank
    seqs, block, width = tokens.shape
    shard = input_weight.shape[0]
    units = down_weight.shape[0]
    head_dim = width // HEADS
    heads = HEADS // seq
    pair = 2 if heads % 2 == 0 else 1
    groups = heads // pair
    lanes = pair * head_dim
    span = heads * head_dim
    place = rank.astype(jnp.int32).reshape(1)

    vectors = (input_bias, output_bias, up_bias, down_bias, attention_gain, attention_shift, feedforward_gain, feedforward_shift)
    wide = 4 * span
    slot = wide // len(vectors)
    dealt = deal(place, input_weight, output_weight, up_weight, vectors, seq, groups, units)
    head_rows, up_rows = gather_heads(
        place, [dealt[0]] + [at.seq_swap(dealt[k], k) for k in range(1, seq)], shard
    )
    tokens_all = at.seq_gather(tokens)
    head_all = at.dp_gather(head_rows)
    up_all = at.dp_gather(up_rows).reshape(width, dp * units)
    down_all = at.dp_gather(after(down_weight, up_rows)).reshape(dp * units, width)
    cot_near = at.seq_gather_near(after(cotangent, *tokens_all[1:]))

    gathered = head_all[:, seq * shard : seq * shard + seq, :]
    bias_in, bias_out, bias_up, bias_down, gain_attn, shift_attn, gain_ff, shift_ff = (
        gathered[:, :, i * slot : i * slot + v.shape[0]].reshape(-1).astype(full)
        for i, v in enumerate(vectors)
    )
    norms = jnp.stack([gain_attn, shift_attn, gain_ff, shift_ff], 0)
    out_split_all = head_all[:, : seq * shard, 3 * span :].reshape(seq, span, span)
    out_all = lay_columns(place, at.seq_exchange(lambda spot: pick(out_split_all, spot, 0)))

    rows = seq * seqs * block
    pieces = [p.reshape(-1, width) for p in tokens_all]
    if seq != 4 or seqs != 1:
        pieces = [jnp.concatenate(pieces, 0)]

    in_bias_mine = jnp.swapaxes(
        pick(bias_in.reshape(3, seq, groups, lanes), rank, 1), 0, 1
    ).reshape(1, 3 * span)
    up_bias_mine = pick(bias_up.reshape(dp, seq, units), rank, 1).reshape(1, dp * units)

    cos_table, sin_table = rotary_tables(seq * block, lanes, head_dim)
    x, normed_attn, normed_ff, qkv = project(
        place, pieces, head_all, in_bias_mine, norms, jnp.asarray(cos_table), jnp.asarray(sin_table),
        block, seqs, lanes, head_dim, seq * shard,
    )
    qkv = qkv.reshape(seq, seqs, block, 3 * span)
    exact, attended, lse = attend(place, qkv, pair, head_dim)
    attended = attended.reshape(rows, span)
    cot_all = at.seq_gather_far(cot_near, attended)

    active, slope = expand(normed_ff, up_all, up_bias_mine, block, (attended, out_all))

    pieces = [p.reshape(-1, width) for p in cot_all]
    if seq != 4 or seqs != 1:
        pieces = [jnp.concatenate(pieces, 0)]
    cot, out_part, attended_grad, hidden_grad, up_bias_sum = turnabout(
        attended, active, slope, out_all, down_all, pieces, block
    )
    out_part = out_part.reshape(seq, seqs, block, width)
    out_near = [at.seq_swap(out_part[k], k) for k in range(1, seq)]

    out_grad = lax.optimization_barrier(contract(attended, cot, 0, 0).astype(low))
    out_pieces = jnp.swapaxes(out_grad.reshape(span, seq, span), 0, 1)
    out_grad = at.seq_trade(out_pieces, place)
    out_grads = at.dp_reduce(out_grad.reshape(dp, seq * shard, span))
    down_grad = contract(active, cot, 0, 0).astype(low)
    up_grad = contract(normed_ff, hidden_grad, 0, 0).astype(low)
    down_grad, up_grad = lax.optimization_barrier((down_grad, up_grad))
    unit_grads = jnp.concatenate(
        [down_grad.reshape(dp, units, width), up_grad.reshape(dp, seq * shard * dp * units // width, width)], 1
    )
    back_wait = (unit_grads, out_grad)
    unit_sum_grads = at.dp_reduce(unit_grads)

    order = [rank ^ k for k in range(seq)]
    tables = [
        jnp.stack([pick(jnp.asarray(t.reshape(seq, block, lanes)), spot, 0) for spot in order], 0)
        for t in (cos_table, sin_table)
    ]
    mixed_grad, in_bias_sum = attend_back(
        place, qkv, exact, attended_grad.reshape(seq, seqs, block, span), lse, *tables, pair, head_dim, back_wait
    )
    mixed_grad = mixed_grad.reshape(rows, 3 * span)
    in_grad = lax.optimization_barrier(contract(normed_attn, mixed_grad, 0, 0).astype(low))
    wait = (in_grad, out_grads, *out_near)
    last = (seq - 1) * seqs
    weights = (head_all, up_all, norms)
    far_grad, far_sums = unproject(x, mixed_grad, hidden_grad, *weights, block, last, seqs, wait)
    near_grad, near_sums = unproject(x, mixed_grad, hidden_grad, *weights, block, seqs, last - seqs, (far_grad,))
    own_grad, own_sums = unproject(x, mixed_grad, hidden_grad, *weights, block, 0, seqs, (near_grad,))
    norm_sums = far_sums + near_sums + own_sums
    near_grad = near_grad.reshape(seq - 2, seqs, block, width)
    _, unit_near = reduce_steps(
        at, far_grad.reshape(seqs, block, width), lambda: [near_grad[k] for k in range(seq - 2)]
    )
    unit_sum = own_grad.reshape(seqs, block, width).astype(full) + sum(a.astype(full) for a in unit_near)
    out_sum = out_part[0].astype(full) + sum(a.astype(full) for a in out_near)
    output = (tokens.astype(full) + out_sum + (bias_out + bias_down)).astype(low)
    unit, rstd = normalised(tokens.astype(full))
    token_grad = cotangent.astype(full) + rstd * (
        unit_sum
        - jnp.mean(unit_sum, axis=-1, keepdims=True)
        - unit * jnp.mean(unit_sum * unit, axis=-1, keepdims=True)
    )
    token_grad = token_grad.astype(low)

    in_bias_sum = jnp.sum(in_bias_sum, axis=0)
    in_bias_sum = jnp.swapaxes(in_bias_sum, 0, 1).reshape(3, 1, span)
    in_bias_sum = lax.dynamic_update_slice_in_dim(jnp.zeros((3, seq, span), full), in_bias_sum, rank, 1)
    up_bias_sum = up_bias_sum.reshape(dp, 1, units)
    up_bias_sum = lax.dynamic_update_slice_in_dim(jnp.zeros((dp, seq, units), full), up_bias_sum, rank, 1)
    out_bias_sum = jnp.sum(cotangent.astype(full), axis=(0, 1))
    in_bias_sum = in_bias_sum.reshape(3 * width)
    small = [
        in_bias_sum[: 2 * width],
        in_bias_sum[2 * width :],
        out_bias_sum,
        up_bias_sum,
        norm_sums[0],
        norm_sums[1],
        norm_sums[2],
        norm_sums[3],
    ]
    small = jnp.concatenate([v.reshape(dp, seq, -1) for v in small], 2)
    lengths = [3 * shard - shard, shard, shard, units, shard, shard, shard, shard]
    edges = np.cumsum([0] + lengths)

    in_grads = at.dp_reduce(after(in_grad.reshape(dp, seq * shard, 3 * span), unit_sum_grads))
    down_final = unit_sum_grads[:units].astype(full)
    up_final = unit_sum_grads[units:].reshape(seq, shard, dp * units)
    up_final = jnp.swapaxes(at.seq_turnover(up_final), 0, 1).reshape(shard, seq, dp, units)
    up_final = jnp.swapaxes(up_final, 1, 2).reshape(shard, dp * seq * units).astype(full)
    in_final = at.seq_turnover(in_grads.reshape(seq, shard, 3 * span)).reshape(seq, shard, groups, 3, lanes)
    in_final = jnp.transpose(in_final, (1, 3, 0, 2, 4)).reshape(shard, 3 * width).astype(full)
    out_final = at.seq_turnover(out_grads.reshape(seq, shard, span))
    out_final = jnp.swapaxes(out_final, 0, 1).reshape(shard, width).astype(full)
    total = at.small_reduce(small)
    (query_key_bias, value_bias, out_bias, up_bias_grad, *norm_grads) = [
        total[edges[i] : edges[i + 1]] for i in range(8)
    ]
    return (
        output,
        token_grad,
        in_final,
        query_key_bias,
        value_bias,
        out_final,
        out_bias,
        up_final,
        up_bias_grad,
        down_final,
        out_bias,
        *norm_grads,
    )


def solution(mesh):
    rows = P(("dp", "seq"), None)
    flat = P(("dp", "seq"))
    held = P("dp", "seq", None)
    return jax.shard_map(
        on_device,
        mesh=mesh,
        in_specs=(held, rows, flat, rows, flat, rows, flat, rows, flat, flat, flat, flat, flat, held),
        out_specs=(held, held, rows, flat, flat, rows, flat, rows, flat, rows, flat, flat, flat, flat, flat),
        check_vma=False,
    )
```

```python
import functools
import math

import jax
import jax.numpy as jnp
import numpy as np
from jax import lax
from jax.experimental import pallas as pl
from jax.experimental.pallas import tpu as pltpu
from jax.sharding import PartitionSpec as P

HEADS = 16
ROT = 16

norm_eps = 1e-05
masked_score = -1e30
low = jnp.bfloat16
full = jnp.float32
kernel_memory = 56 * 1024 * 1024


def place_at(pieces, spots, axis):
    count = len(pieces)
    shape = list(pieces[0].shape)
    shape.insert(axis, count)
    held = jnp.zeros(shape, pieces[0].dtype)
    for piece, spot in zip(pieces, spots):
        held = lax.dynamic_update_index_in_dim(held, piece, spot, axis)
    return held


def pick(array, spot, axis):
    return lax.dynamic_index_in_dim(array, spot, axis, keepdims=False)


def effort(micros):
    return pl.CostEstimate(flops=int(micros * 1.1e9), bytes_accessed=1, transcendentals=0)


anywhere = pl.BlockSpec(memory_space=pl.ANY)


def pass_kernel(*refs):
    del refs


def after_big(array, *others):
    return pl.pallas_call(
        pass_kernel,
        in_specs=[anywhere] * (1 + len(others)),
        out_specs=anywhere,
        out_shape=jax.ShapeDtypeStruct(array.shape, array.dtype),
        input_output_aliases={0: 0},
        name="after_big",
    )(array, *others)


def join_kernel(first, second, *refs):
    rows = first.shape[0]
    refs[-1][:rows, :] = first[...]
    refs[-1][rows:, :] = second[...]


def join(first, second, wait):
    vmem = pl.BlockSpec(memory_space=pltpu.VMEM)
    return pl.pallas_call(
        join_kernel,
        in_specs=[vmem, vmem] + [anywhere] * len(wait),
        out_specs=vmem,
        out_shape=jax.ShapeDtypeStruct((first.shape[0] + second.shape[0], first.shape[1]), first.dtype),
        compiler_params=pltpu.CompilerParams(vmem_limit_bytes=kernel_memory),
        name="join",
    )(first, second, *wait)


def after_kernel(source, *refs):
    refs[-1][...] = source[...]


def after(array, *others):
    vmem = pl.BlockSpec(memory_space=pltpu.VMEM)
    return pl.pallas_call(
        after_kernel,
        in_specs=[vmem] + [anywhere] * len(others),
        out_specs=vmem,
        out_shape=jax.ShapeDtypeStruct(array.shape, array.dtype),
        compiler_params=pltpu.CompilerParams(vmem_limit_bytes=kernel_memory),
        name="after",
    )(array, *others)


def chosen_units(ref, rank, ranks, units):
    runs = ref.shape[1] // (ranks * units)
    parts = []
    for run in range(runs):
        first = run * ranks * units
        if units % 128 == 0:
            parts.append(ref[:, pl.ds(pl.multiple_of(first + rank * units, 128), units)])
        else:
            whole = ref[:, first : first + ranks * units]
            part = jnp.zeros((ref.shape[0], units), ref.dtype)
            for r in range(ranks):
                part = jnp.where(rank == r, whole[:, r * units : (r + 1) * units], part)
            parts.append(part)
    return jnp.concatenate(parts, 1)


def deal_kernel(ranks, groups, vectors, units, place, in_ref, up_ref, *refs):
    shard, columns = in_ref.shape
    width = columns // 3
    span = width // ranks
    lanes = span // groups
    for k in range(ranks):
        rank = place[0] ^ k
        dealt = refs[vectors + k]
        dealt[:shard, 3 * span :] = jnp.zeros((shard, span), low)

        def part(start):
            first = start + rank * span
            if span % 128 == 0:
                return in_ref[:, pl.ds(pl.multiple_of(first, 128), span)]
            whole = in_ref[:, start : start + width]
            chosen = jnp.zeros((shard, span), low)
            for r in range(ranks):
                chosen = jnp.where(rank == r, whole[:, r * span : (r + 1) * span], chosen)
            return chosen

        for kind in range(3):
            mine = part(kind * width)
            for group in range(groups):
                target = (group * 3 + kind) * lanes
                dealt[:shard, target : target + lanes] = mine[:, group * lanes : (group + 1) * lanes]
        dealt[shard + 16 :, :] = chosen_units(up_ref, rank, ranks, units)
        dealt[shard : shard + 16, :] = jnp.zeros((16, 4 * span), low)
        for i, ref in enumerate(refs[:vectors]):
            dealt[shard + i : shard + i + 1, : ref.shape[1]] = ref[...]


def deal(place, input_weight, up_weight, vectors, ranks, groups, units):
    shard, columns = input_weight.shape
    arrays = [input_weight, up_weight] + [v[None] for v in vectors]
    shape = (2 * shard + 16, 4 * columns // (3 * ranks))
    vmem = pl.BlockSpec(memory_space=pltpu.VMEM)
    return pl.pallas_call(
        functools.partial(deal_kernel, ranks, groups, len(vectors), units),
        in_specs=[pl.BlockSpec(memory_space=pltpu.SMEM)] + [vmem] * len(arrays),
        out_specs=[vmem] * ranks,
        out_shape=[jax.ShapeDtypeStruct(shape, low)] * ranks,
        compiler_params=pltpu.CompilerParams(vmem_limit_bytes=kernel_memory),
        name="deal",
    )(place, *arrays)


def gather_heads_kernel(count, shard, place, *refs):
    out, units = refs[count:]
    columns = out.shape[1]
    for k in range(count):
        rank = place[0] ^ k
        if shard % 16 == 0:
            here = pl.ds(pl.multiple_of(rank * shard, 16), shard)
            out[here, :] = refs[k][:shard, :columns]
            units[here, :] = refs[k][shard + 16 :, :]
        else:
            for r in range(count):

                @pl.when(rank == r)
                def _(r=r, k=k):
                    out[r * shard : (r + 1) * shard, :] = refs[k][:shard, :columns]
                    units[r * shard : (r + 1) * shard, :] = refs[k][shard + 16 :, :]

    vectors = []
    for r in range(count):
        mine = jnp.zeros((8, columns), full)
        for k in range(count):
            rows = refs[k][shard : shard + 16, :columns].astype(full)[:8]
            mine = jnp.where((place[0] ^ k) == r, rows, mine)
        vectors.append(mine)
    out[count * shard :, :] = jnp.concatenate(vectors, 0).astype(low)


def gather_heads(place, pieces, shard):
    count = len(pieces)
    wide = pieces[0].shape[1]
    vmem = pl.BlockSpec(memory_space=pltpu.VMEM)
    return pl.pallas_call(
        functools.partial(gather_heads_kernel, count, shard),
        in_specs=[pl.BlockSpec(memory_space=pltpu.SMEM)] + [vmem] * count,
        out_specs=[vmem, vmem],
        out_shape=[
            jax.ShapeDtypeStruct((count * shard + count * 8, wide // 4 * 3), low),
            jax.ShapeDtypeStruct((count * shard, wide), low),
        ],
        compiler_params=pltpu.CompilerParams(vmem_limit_bytes=kernel_memory),
        name="gather_heads",
    )(place, *pieces)


def cut_kernel(x_ref, y_ref, *refs):
    first, second = refs[-2:]
    first[...] = x_ref[...]
    second[...] = y_ref[...]


def cut(x, y, wait):
    seqs, block, width = x.shape
    half = (seqs, block // 2, width)
    return pl.pallas_call(
        cut_kernel,
        grid=(1,),
        in_specs=[pl.BlockSpec(half, lambda i: (0, 0, 0)), pl.BlockSpec(half, lambda i: (0, 1, 0))]
        + [anywhere] * len(wait),
        out_specs=[pl.BlockSpec(half, lambda i: (0, 0, 0))] * 2,
        out_shape=[jax.ShapeDtypeStruct(half, x.dtype)] * 2,
        compiler_params=pltpu.CompilerParams(vmem_limit_bytes=kernel_memory),
        name="cut",
    )(x, y, *wait)


def lay_columns_kernel(count, place, *refs):
    out = refs[count]
    span = refs[0].shape[1]
    for k in range(count):
        rank = place[0] ^ k
        if span % 128 == 0:
            out[:, pl.ds(pl.multiple_of(rank * span, 128), span)] = refs[k][...]
        else:
            for r in range(count):

                @pl.when(rank == r)
                def _(r=r, k=k):
                    out[:, r * span : (r + 1) * span] = refs[k][...]


def lay_columns(place, pieces):
    count = len(pieces)
    rows, span = pieces[0].shape
    vmem = pl.BlockSpec(memory_space=pltpu.VMEM)
    return pl.pallas_call(
        functools.partial(lay_columns_kernel, count),
        in_specs=[pl.BlockSpec(memory_space=pltpu.SMEM)] + [vmem] * count,
        out_specs=vmem,
        out_shape=jax.ShapeDtypeStruct((rows, count * span), pieces[0].dtype),
        compiler_params=pltpu.CompilerParams(vmem_limit_bytes=kernel_memory),
        name="lay_columns",
    )(place, *pieces)


def lay_kernel(count, place, *refs):
    out = refs[count]
    for k in range(count):
        out[place[0] ^ k] = refs[k][...]


def lay(place, pieces):
    count = len(pieces)
    shape = (count,) + pieces[0].shape
    return pl.pallas_call(
        functools.partial(lay_kernel, count),
        grid_spec=pltpu.PrefetchScalarGridSpec(
            num_scalar_prefetch=1,
            grid=(1,),
            in_specs=[pl.BlockSpec(p.shape, lambda i, place, n=p.ndim: (0,) * n) for p in pieces],
            out_specs=pl.BlockSpec(shape, lambda i, place: (0,) * len(shape)),
        ),
        out_shape=jax.ShapeDtypeStruct(shape, pieces[0].dtype),
        compiler_params=pltpu.CompilerParams(vmem_limit_bytes=kernel_memory),
        name="lay",
    )(place, *pieces)


class Layout:
    def __init__(self):
        self.dp = lax.axis_size("dp")
        self.seq = lax.axis_size("seq")
        self.rank = lax.axis_index("seq")

    def seq_swap(self, array, k):
        return lax.ppermute(array, "seq", [(i, i ^ k) for i in range(self.seq)])

    def to_heads(self, array):
        pairs = [(f, (f % self.dp) * self.seq + f // self.dp) for f in range(self.dp * self.seq)]
        return lax.ppermute(array, ("dp", "seq"), pairs)

    def from_heads(self, array):
        pairs = [((f % self.dp) * self.seq + f // self.dp, f) for f in range(self.dp * self.seq)]
        return lax.ppermute(array, ("dp", "seq"), pairs)

    def seq_exchange(self, piece_for):
        return [piece_for(self.rank)] + [
            self.seq_swap(piece_for(self.rank ^ k), k) for k in range(1, self.seq)
        ]

    def seq_trade(self, array, place):
        return lay(place, self.seq_exchange(lambda spot: pick(array, spot, 0)))

    def seq_spots(self):
        return [self.rank ^ k for k in range(self.seq)]

    def seq_gather_direct(self, array):
        return [array] + [self.seq_swap(array, k) for k in range(1, self.seq)]

    def seq_gather(self, array):
        if self.seq != 4:
            return self.seq_gather_direct(array)
        return self.seq_gather_far(self.seq_gather_near(array))

    def seq_gather_near(self, array):
        if self.seq != 4:
            return self.seq_gather_direct(array)
        return [array, self.seq_swap(array, 1), self.seq_swap(array, 2)]

    def seq_gather_far(self, near, *wait):
        if self.seq != 4:
            return near
        first, second = cut(near[1], near[2], wait)
        return near + [self.seq_swap(first, 2), self.seq_swap(second, 1)]

    def seq_reduce_far(self, part):
        half = part.shape[1] // 2
        return self.seq_swap(part[:, half:], 2), self.seq_swap(part[:, :half], 1)

    def seq_reduce_near(self, parts, far):
        half = parts[0].shape[1] // 2
        for_x, for_y = (a.astype(full) for a in far)
        p1, p2 = parts
        p1 = jnp.concatenate([p1[:, :half], (p1[:, half:].astype(full) + for_x).astype(low)], 1)
        p2 = jnp.concatenate([(p2[:, :half].astype(full) + for_y).astype(low), p2[:, half:]], 1)
        return self.seq_swap(p1, 1), self.seq_swap(p2, 2)

    def seq_turnover(self, array):
        return lax.all_to_all(array, "seq", 0, 0, tiled=True)

    def z_turn(self, array, k):
        return lax.ppermute(array, "dp", [(i, (i + k) % self.dp) for i in range(self.dp)])

    def small_reduce(self, array):
        array = sum(self.seq_exchange(lambda spot: pick(array, spot, 1)))
        cores = 2 if self.dp % 2 == 0 else 1
        here = lax.axis_index("dp")
        core, z = here % cores, here // cores
        line = self.dp // cores
        pairs = array.reshape((line, cores) + array.shape[1:])
        if cores == 2:
            swap = [(i, i ^ 1) for i in range(self.dp)]
            array = pick(pairs, core, 1) + lax.ppermute(pick(pairs, 1 - core, 1), "dp", swap)
        else:
            array = pairs[:, 0]
        total = pick(array, z, 0)
        for k in range(1, line):
            total = total + self.z_turn(pick(array, (z + k) % line, 0), k * cores)
        return total

    def dp_gather(self, array):
        return lax.all_gather(array, "dp", axis=0, tiled=False)

    def dp_reduce(self, array):
        return lax.psum_scatter(array, "dp", scatter_dimension=0, tiled=False)


def rotary_tables(length, lanes, head_dim):
    half = ROT // 2
    exponent = -np.arange(0, ROT, 2, dtype=np.float32) / np.float32(ROT)
    frequency = np.float32(10000.0) ** exponent
    phase = np.arange(length, dtype=np.float32)[:, None] * frequency[None, :]
    cosine = np.ones((length, head_dim), np.float32)
    sine = np.zeros((length, head_dim), np.float32)
    cosine[:, :half] = cosine[:, half:ROT] = np.cos(phase)
    sine[:, :half] = -np.sin(phase)
    sine[:, half:ROT] = np.sin(phase)
    copies = lanes // head_dim
    return np.tile(cosine, (1, copies)), np.tile(sine, (1, copies))


def roll_lanes(x, shift):
    size = x.shape[-1]
    if size % 128 == 0:
        return pltpu.roll(x, shift % size, x.ndim - 1)
    return jnp.roll(x, shift, -1)


def turn(x, cosine, sine, head_dim):
    half = ROT // 2
    lane = lax.broadcasted_iota(jnp.int32, x.shape, 1) % head_dim
    swapped = jnp.where(lane < half, roll_lanes(x, -half), roll_lanes(x, half))
    return x * cosine + swapped * sine


def normalised(x):
    mean = jnp.mean(x, axis=-1, keepdims=True)
    centered = x - mean
    variance = jnp.mean(centered * centered, axis=-1, keepdims=True)
    rstd = lax.rsqrt(variance + norm_eps)
    return centered * rstd, rstd


def project_kernel(head_dim, lanes, shard, columns, stacked, count, place, head_ref, bias_ref, norms_ref, cos_ref, sin_ref, *refs):
    pieces, (x_out, attn_ref, ff_ref, qkv_ref, weight_ref) = refs[:count], refs[-5:]
    block, width = x_out.shape
    step = pl.program_id(0)

    @pl.when(step == 0)
    def _():
        weight_ref[...] = head_ref[:, :shard, :columns].reshape(width, columns)

    if stacked:
        x_out[...] = pieces[0][...]
    else:
        first = 0
        for piece in pieces:
            rows = piece.shape[0]
            inside = first % block

            @pl.when(step == first // block)
            def _(piece=piece, inside=inside, rows=rows):
                x_out[inside : inside + rows, :] = piece[...]

            first += rows
    unit, _ = normalised(x_out[...].astype(full))
    normed = (unit * norms_ref[0:1, :] + norms_ref[1:2, :]).astype(low)
    attn_ref[...] = normed
    ff_ref[...] = (unit * norms_ref[2:3, :] + norms_ref[3:4, :]).astype(low)
    mixed = jnp.dot(normed, weight_ref[...], preferred_element_type=full) + bias_ref[...]
    cosine, sine = cos_ref[...], sin_ref[...]
    for group in range(columns // lanes):
        span = slice(group * lanes, (group + 1) * lanes)
        part = mixed[:, span]
        if group % 3 < 2:
            part = turn(part, cosine, sine, head_dim)
        qkv_ref[:, span] = part.astype(low)


def project(place, pieces, head, bias, norms, cosine, sine, block, seqs, lanes, head_dim, shard, rows, start=0, earlier=()):
    stacked = len(pieces) == 1
    width = pieces[0].shape[1]
    columns = bias.shape[1]
    whole = lambda i, place: (0, 0)
    step = lambda i, place: (i + start, 0)
    spot = lambda i, place: (((i + start) // seqs) ^ place[0], 0)
    if stacked:
        piece_specs = [pl.BlockSpec((block, width), step)]
    else:
        piece_specs = [pl.BlockSpec(p.shape, whole) for p in pieces]
    return pl.pallas_call(
        functools.partial(project_kernel, head_dim, lanes, shard, columns, stacked, len(pieces)),
        grid_spec=pltpu.PrefetchScalarGridSpec(
            num_scalar_prefetch=1,
            grid=(sum(p.shape[0] for p in pieces) // block,),
            in_specs=[
                pl.BlockSpec(head.shape, lambda i, place: (0, 0, 0)),
                pl.BlockSpec((1, columns), whole),
                pl.BlockSpec((4, width), whole),
                pl.BlockSpec((block, lanes), spot),
                pl.BlockSpec((block, lanes), spot),
            ]
            + piece_specs
            + [anywhere] * len(earlier),
            out_specs=[
                pl.BlockSpec((block, width), step),
                pl.BlockSpec((block, width), step),
                pl.BlockSpec((block, width), step),
                pl.BlockSpec((block, columns), step),
            ],
            scratch_shapes=[pltpu.VMEM((width, columns), low)],
        ),
        out_shape=[
            jax.ShapeDtypeStruct((rows, width), low),
            jax.ShapeDtypeStruct((rows, width), low),
            jax.ShapeDtypeStruct((rows, width), low),
            jax.ShapeDtypeStruct((rows, columns), low),
        ],
        input_output_aliases={6 + len(pieces) + i: i for i in range(len(earlier))},
        compiler_params=pltpu.CompilerParams(vmem_limit_bytes=kernel_memory),
        cost_estimate=effort(12 * sum(p.shape[0] for p in pieces) / 2048),
        name="project",
    )(place, head, bias, norms, cosine, sine, *pieces, *earlier)


def contract(a, b, da, db):
    return lax.dot_general(a, b, (((da,), (db,)), ((), ())), preferred_element_type=full)


def head_lanes(x, head, pair, head_dim):
    if pair == 1:
        return x
    lane = lax.broadcasted_iota(jnp.int32, x.shape, 1)
    inside = (lane >= head * head_dim) & (lane < (head + 1) * head_dim)
    return jnp.where(inside, x, jnp.zeros_like(x))


def attend_kernel(pair, head_dim, place, qkv_ref, exact_ref, low_ref, lse_ref):
    count, block, lanes3 = qkv_ref.shape
    lanes = lanes3 // 3
    scale = 1.0 / math.sqrt(head_dim)
    s = place[0]
    row = lax.broadcasted_iota(jnp.int32, (block, block), 0)
    column = lax.broadcasted_iota(jnp.int32, (block, block), 1)
    for i in range(count):
        here = i ^ s
        query = qkv_ref[here, :, 0:lanes] * jnp.asarray(scale, low)
        joined = jnp.zeros((block, lanes), full)
        for head in range(pair):
            mine = head_lanes(query, head, pair, head_dim)
            scores = []
            for j in range(i + 1):
                part = contract(mine, qkv_ref[j ^ s, :, lanes : 2 * lanes], 1, 1)
                if j == i:
                    part = jnp.where(column <= row, part, masked_score)
                scores.append(part)
            top = functools.reduce(jnp.maximum, scores)
            top = jnp.max(top, axis=-1, keepdims=True)
            total = None
            update = None
            for j in range(i + 1):
                weights = jnp.exp(scores[j] - top)
                term = jnp.dot(
                    weights.astype(low), qkv_ref[j ^ s, :, 2 * lanes :], preferred_element_type=full
                )
                update = term if update is None else update + term
                total = weights if total is None else total + weights
            total = jnp.sum(total, axis=-1, keepdims=True)
            joined = joined + head_lanes(update / total, head, pair, head_dim)
            lse = jnp.broadcast_to(top + jnp.log(total), (block, 128))
            lse_ref[here, head : head + 1, :] = jnp.transpose(lse)[0:1, :]
        exact_ref[here] = joined
        low_ref[here] = joined.astype(low)


def attend(place, qkv, pair, head_dim):
    count, seqs, block, columns = qkv.shape
    lanes = pair * head_dim
    groups = columns // (3 * lanes)
    spec = lambda width: pl.BlockSpec((count, None, block, width), lambda b, g, place: (0, b, 0, g))
    return pl.pallas_call(
        functools.partial(attend_kernel, pair, head_dim),
        grid_spec=pltpu.PrefetchScalarGridSpec(
            num_scalar_prefetch=1,
            grid=(seqs, groups),
            in_specs=[spec(3 * lanes)],
            out_specs=[
                spec(lanes),
                spec(lanes),
                pl.BlockSpec((count, None, None, pair, block), lambda b, g, place: (0, b, g, 0, 0)),
            ],
        ),
        out_shape=[
            jax.ShapeDtypeStruct((count, seqs, block, groups * lanes), full),
            jax.ShapeDtypeStruct((count, seqs, block, groups * lanes), low),
            jax.ShapeDtypeStruct((count, seqs, groups, pair, block), full),
        ],
        compiler_params=pltpu.CompilerParams(vmem_limit_bytes=kernel_memory),
        cost_estimate=effort(18 * seqs * groups / 2),
        name="attend",
    )(place, qkv)


def attend_back_kernel(pair, head_dim, place, qkv_ref, exact_ref, grad_ref, lse_ref, cos_ref, sin_ref, *refs):
    out_ref, key_ref, value_ref = refs[-3:]
    count, block, lanes3 = qkv_ref.shape
    lanes = lanes3 // 3
    scale = 1.0 / math.sqrt(head_dim)
    s = place[0]
    row = lax.broadcasted_iota(jnp.int32, (block, block), 0)
    column = lax.broadcasted_iota(jnp.int32, (block, block), 1)
    key_ref[...] = jnp.zeros_like(key_ref)
    value_ref[...] = jnp.zeros_like(value_ref)

    def back(total, at):
        kept = total.astype(low).astype(full)
        return turn(kept, cos_ref[at], -sin_ref[at], head_dim).astype(low)

    for i in range(count):
        here = i ^ s
        query = qkv_ref[here, :, 0:lanes] * jnp.asarray(scale, low)
        grad = grad_ref[here]
        product = exact_ref[here] * grad.astype(full)
        joined = jnp.zeros((block, lanes), full)
        for head in range(pair):
            mine = head_lanes(query, head, pair, head_dim)
            mine_grad = head_lanes(grad, head, pair, head_dim)
            delta = jnp.sum(
                jnp.transpose(head_lanes(product, head, pair, head_dim)), axis=0, keepdims=True
            )
            lse = lse_ref[here, head : head + 1, :]
            update = None
            for j in range(i + 1):
                there = j ^ s
                key = qkv_ref[there, :, lanes : 2 * lanes]
                value = qkv_ref[there, :, 2 * lanes :]
                scores = contract(key, mine, 1, 1)
                if j == i:
                    scores = jnp.where(row <= column, scores, masked_score)
                probs = jnp.exp(scores - lse)
                prob_grad = contract(value, mine_grad, 1, 1)
                score_grad = (probs * (prob_grad - delta)).astype(low)
                value_ref[j] += jnp.dot(probs.astype(low), mine_grad, preferred_element_type=full)
                key_ref[j] += jnp.dot(score_grad, mine, preferred_element_type=full)
                term = contract(score_grad, key, 0, 0)
                update = term if update is None else update + term
            joined = joined + head_lanes(update, head, pair, head_dim)
        out_ref[here, :, 0:lanes] = back(joined * scale, i)
    for j in range(count):
        there = j ^ s
        out_ref[there, :, lanes : 2 * lanes] = back(key_ref[j], j)
        out_ref[there, :, 2 * lanes :] = value_ref[j].astype(low)


def attend_back(place, qkv, exact, grad, lse, cosine, sine, pair, head_dim, wait):
    count, seqs, block, columns = qkv.shape
    lanes = pair * head_dim
    groups = columns // (3 * lanes)
    spec = lambda width: pl.BlockSpec((count, None, block, width), lambda b, g, place: (0, b, 0, g))
    table = pl.BlockSpec((count, block, lanes), lambda b, g, place: (0, 0, 0))
    return pl.pallas_call(
        functools.partial(attend_back_kernel, pair, head_dim),
        grid_spec=pltpu.PrefetchScalarGridSpec(
            num_scalar_prefetch=1,
            grid=(seqs, groups),
            in_specs=[
                spec(3 * lanes),
                spec(lanes),
                spec(lanes),
                pl.BlockSpec((count, None, None, pair, block), lambda b, g, place: (0, b, g, 0, 0)),
                table,
                table,
            ]
            + [anywhere] * len(wait),
            out_specs=spec(3 * lanes),
            scratch_shapes=[
                pltpu.VMEM((count, block, lanes), full),
                pltpu.VMEM((count, block, lanes), full),
            ],
        ),
        out_shape=jax.ShapeDtypeStruct(qkv.shape, low),
        compiler_params=pltpu.CompilerParams(vmem_limit_bytes=kernel_memory),
        cost_estimate=effort(33 * seqs * groups / 2),
        name="attend_back",
    )(place, qkv, exact, grad, lse, cosine, sine, *wait)


def expand_kernel(x_ref, weight_ref, bias_ref, *refs):
    active_ref, slope_ref = refs[-2:]
    hidden = jnp.dot(x_ref[...], weight_ref[...], preferred_element_type=full) + bias_ref[...]
    tail = 0.5 * (1.0 + lax.erf(hidden * np.float32(math.sqrt(0.5))))
    bell = jnp.exp(-0.5 * hidden * hidden) * np.float32(1.0 / math.sqrt(2.0 * math.pi))
    active_ref[...] = (hidden * tail).astype(low)
    slope_ref[...] = (tail + hidden * bell).astype(low)


def expand(x, weight, bias, block, wait):
    rows, width = x.shape
    columns = weight.shape[1]
    whole = lambda i: (0, 0)
    step = lambda i: (i, 0)
    return pl.pallas_call(
        expand_kernel,
        grid=(rows // block,),
        in_specs=[
            pl.BlockSpec((block, width), step),
            pl.BlockSpec((width, columns), whole),
            pl.BlockSpec((1, columns), whole),
        ]
        + [anywhere] * len(wait),
        out_specs=[pl.BlockSpec((block, columns), step), pl.BlockSpec((block, columns), step)],
        out_shape=[jax.ShapeDtypeStruct((rows, columns), low)] * 2,
        compiler_params=pltpu.CompilerParams(vmem_limit_bytes=kernel_memory),
        cost_estimate=effort(12 * rows / 2048),
        name="expand",
    )(x, weight, bias, *wait)


def turnabout_kernel(stacked, count, units, attended_ref, active_ref, slope_ref, back_ref, *refs):
    pieces, parts = refs[:count], refs[count:-6]
    cot_ref, attended_grad_ref, hidden_grad_ref, sum_ref, down_ref, out_ref = refs[-6:]
    block, width = cot_ref.shape
    step = pl.program_id(0)

    @pl.when(step == 0)
    def _():
        down_ref[...] = back_ref[:, :units, :].reshape(down_ref.shape)
        out_ref[...] = back_ref[:, units:, :].reshape(out_ref.shape)

    down, out = down_ref[...], out_ref[...]
    part = jnp.dot(attended_ref[...], out, preferred_element_type=full)
    part = part + jnp.dot(active_ref[...], down, preferred_element_type=full)
    part = part.astype(low)
    if stacked:
        cot_ref[...] = pieces[0][...]
        parts[0][...] = part
    else:
        for k, ref in enumerate(parts):

            @pl.when(step == k)
            def _(ref=ref):
                ref[...] = part

        first = 0
        for piece in pieces:
            rows = piece.shape[0]
            inside = first % block

            @pl.when(step == first // block)
            def _(piece=piece, inside=inside, rows=rows):
                cot_ref[inside : inside + rows, :] = piece[...]

            first += rows
    cot = cot_ref[...]
    attended_grad_ref[...] = contract(cot, out, 1, 1).astype(low)
    hidden = (contract(cot, down, 1, 1) * slope_ref[...].astype(full)).astype(low)
    hidden_grad_ref[...] = hidden
    total = jnp.sum(hidden.astype(full), axis=0, keepdims=True)

    @pl.when(step == 0)
    def _():
        sum_ref[...] = total

    @pl.when(step > 0)
    def _():
        sum_ref[...] += total


def turnabout(attended, active, slope, back_weights, pieces, block, units):
    stacked = len(pieces) == 1
    rows, span = attended.shape
    columns, width = active.shape[1], back_weights.shape[2]
    whole = lambda i: (0, 0)
    step = lambda i: (i, 0)
    if stacked:
        piece_specs = [pl.BlockSpec((block, width), step)]
        part_specs = piece_specs
        part_shapes = [jax.ShapeDtypeStruct((rows, width), low)]
    else:
        piece_specs = [pl.BlockSpec(p.shape, whole) for p in pieces]
        part_specs = [pl.BlockSpec((block, width), whole)] * (rows // block)
        part_shapes = [jax.ShapeDtypeStruct((block, width), low)] * (rows // block)
    *parts, cot, attended_grad, hidden_grad, total = pl.pallas_call(
        functools.partial(turnabout_kernel, stacked, len(pieces), units),
        grid=(rows // block,),
        in_specs=[
            pl.BlockSpec((block, span), step),
            pl.BlockSpec((block, columns), step),
            pl.BlockSpec((block, columns), step),
            pl.BlockSpec(back_weights.shape, lambda i: (0, 0, 0)),
        ]
        + piece_specs,
        out_specs=part_specs
        + [
            pl.BlockSpec((block, width), step),
            pl.BlockSpec((block, span), step),
            pl.BlockSpec((block, columns), step),
            pl.BlockSpec((1, columns), whole),
        ],
        out_shape=part_shapes
        + [
            jax.ShapeDtypeStruct((rows, width), low),
            jax.ShapeDtypeStruct((rows, span), low),
            jax.ShapeDtypeStruct((rows, columns), low),
            jax.ShapeDtypeStruct((1, columns), full),
        ],
        scratch_shapes=[pltpu.VMEM((columns, width), low), pltpu.VMEM((span, width), low)],
        compiler_params=pltpu.CompilerParams(vmem_limit_bytes=kernel_memory),
        cost_estimate=effort(14 * rows / 2048),
        name="turnabout",
    )(attended, active, slope, back_weights, *pieces)
    return parts, cot, attended_grad, hidden_grad, total


def outer_kernel(count, *refs):
    out_ref = refs[2 * count]
    for which in range(count):

        @pl.when(pl.program_id(0) == which)
        def _(which=which):
            got = contract(refs[2 * which][...], refs[2 * which + 1][...], 0, 0)
            out_ref[...] = got.astype(low).reshape(out_ref.shape)


def outer(pairs, parts, halves):
    count = len(pairs)
    rows, columns = pairs[0][0].shape
    width = pairs[0][1].shape[1]
    units = columns // parts
    specs, arrays = [], []
    for which, (a, b) in enumerate(pairs):
        mine = lambda w, h, which=which: (0, jnp.where(w == which, h, jnp.where(w < which, 0, halves - 1)))
        specs += [pl.BlockSpec((rows, columns // halves), mine), pl.BlockSpec((rows, width), lambda w, h: (0, 0))]
        arrays += [a, b]
    return pl.pallas_call(
        functools.partial(outer_kernel, count),
        grid=(count, halves),
        in_specs=specs,
        out_specs=pl.BlockSpec((parts // halves, units, width), lambda w, h: (h, w, 0)),
        out_shape=jax.ShapeDtypeStruct((parts, count * units, width), low),
        compiler_params=pltpu.CompilerParams(vmem_limit_bytes=kernel_memory),
        cost_estimate=effort(5 * count * rows * columns * width / 2**31),
        name="outer",
    )(*arrays)


def hand_kernel(count, moves, place, *refs):
    out = refs[count]
    for k in range(count):
        rank = place[0] ^ k
        for source, target, stride, size in moves:
            piece = refs[k][:, source : source + size].astype(full)
            if size % 128 == 0 and stride % 128 == 0:
                out[:, pl.ds(pl.multiple_of(target + rank * stride, 128), size)] = piece
            else:
                for r in range(count):

                    @pl.when(rank == r)
                    def _(r=r, piece=piece, target=target, stride=stride, size=size):
                        out[:, target + r * stride : target + r * stride + size] = piece


def hand(place, pieces, moves):
    count = len(pieces)
    rows, columns = pieces[0].shape
    vmem = pl.BlockSpec(memory_space=pltpu.VMEM)
    return pl.pallas_call(
        functools.partial(hand_kernel, count, moves),
        in_specs=[pl.BlockSpec(memory_space=pltpu.SMEM)] + [vmem] * count,
        out_specs=vmem,
        out_shape=jax.ShapeDtypeStruct((rows, count * columns), full),
        compiler_params=pltpu.CompilerParams(vmem_limit_bytes=kernel_memory),
        name="hand",
    )(place, *pieces)


def finish_kernel(x_ref, cot_ref, own_ref, first_ref, second_ref, *refs):
    unit, rstd = normalised(x_ref[...].astype(full))
    total = own_ref[...].astype(full) + first_ref[...].astype(full) + second_ref[...].astype(full)
    shift = jnp.mean(total, axis=-1, keepdims=True)
    tilt = jnp.mean(total * unit, axis=-1, keepdims=True)
    refs[-1][...] = (cot_ref[...].astype(full) + rstd * (total - shift - unit * tilt)).astype(low)


def finish(x, cot, own, first, second, wait):
    rows, width = x.shape
    block = rows // 4 if rows % 64 == 0 else rows
    spec = pl.BlockSpec((block, width), lambda i: (i, 0))
    return pl.pallas_call(
        finish_kernel,
        grid=(rows // block,),
        in_specs=[spec] * 5 + [anywhere] * len(wait),
        out_specs=spec,
        out_shape=jax.ShapeDtypeStruct((rows, width), low),
        compiler_params=pltpu.CompilerParams(vmem_limit_bytes=kernel_memory),
        cost_estimate=effort(3 * rows / 512),
        name="finish",
    )(x, cot, own, first, second, *wait)


def unproject_kernel(x_ref, mixed_ref, hidden_ref, in_ref, up_ref, norms_ref, *refs):
    out_ref, sums_ref = refs[-2:]
    unit, _ = normalised(x_ref[...].astype(full))
    width, columns = x_ref.shape[1], mixed_ref.shape[1]
    in_weight = in_ref[:, : width // in_ref.shape[0], :columns].reshape(width, columns)
    attn = contract(mixed_ref[...], in_weight, 1, 1)
    ff = contract(hidden_ref[...], up_ref[...], 1, 1)
    out_ref[...] = (attn * norms_ref[0:1, :] + ff * norms_ref[2:3, :]).astype(low)
    sums = [attn * unit, attn, ff * unit, ff]
    sums = jnp.concatenate([jnp.sum(a, axis=0, keepdims=True) for a in sums], 0)

    @pl.when(pl.program_id(0) == 0)
    def _():
        sums_ref[...] = sums

    @pl.when(pl.program_id(0) > 0)
    def _():
        sums_ref[...] += sums


def unproject(x, mixed, hidden, in_weight, up_weight, norms, block, first, count, wait):
    rows, width = count * block, x.shape[1]
    whole = lambda i: (0, 0)
    step = lambda i: (i + first, 0)
    here = lambda i: (i, 0)
    return pl.pallas_call(
        unproject_kernel,
        grid=(rows // block,),
        in_specs=[
            pl.BlockSpec((block, width), step),
            pl.BlockSpec((block, mixed.shape[1]), step),
            pl.BlockSpec((block, hidden.shape[1]), step),
            pl.BlockSpec(in_weight.shape, lambda i: (0, 0, 0)),
            pl.BlockSpec(up_weight.shape, whole),
            pl.BlockSpec((4, width), whole),
        ]
        + [anywhere] * len(wait),
        out_specs=[pl.BlockSpec((block, width), here), pl.BlockSpec((4, width), whole)],
        out_shape=[
            jax.ShapeDtypeStruct((rows, width), low),
            jax.ShapeDtypeStruct((4, width), full),
        ],
        compiler_params=pltpu.CompilerParams(vmem_limit_bytes=kernel_memory),
        cost_estimate=effort(18 * rows / 2048),
        name="unproject",
    )(x, mixed, hidden, in_weight, up_weight, norms, *wait)


def reduce_steps(at, far, near):
    if at.seq != 4:
        got = [at.seq_swap(a, k + 1) for k, a in enumerate(near())]
        return [], got + [at.seq_swap(far, at.seq - 1)]
    first = at.seq_reduce_far(far)
    return first, list(at.seq_reduce_near(near(), first))


def on_device(
    tokens,
    input_weight,
    input_bias,
    output_weight,
    output_bias,
    up_weight,
    up_bias,
    down_weight,
    down_bias,
    attention_gain,
    attention_shift,
    feedforward_gain,
    feedforward_shift,
    cotangent,
):
    at = Layout()
    dp, seq, rank = at.dp, at.seq, at.rank
    seqs, block, width = tokens.shape
    shard = input_weight.shape[0]
    units = down_weight.shape[0]
    head_dim = width // HEADS
    heads = HEADS // seq
    pair = 2 if heads % 2 == 0 else 1
    groups = heads // pair
    lanes = pair * head_dim
    span = heads * head_dim
    place = rank.astype(jnp.int32).reshape(1)

    vectors = (input_bias, output_bias, up_bias, down_bias, attention_gain, attention_shift, feedforward_gain, feedforward_shift)
    dealt = deal(place, input_weight, up_weight, vectors, seq, groups, units)
    head_rows, up_rows = gather_heads(
        place, [dealt[0]] + [at.seq_swap(dealt[k], k) for k in range(1, seq)], shard
    )
    out_rows = at.to_heads(output_weight)
    tokens_all = at.seq_gather(tokens)
    head_all = at.dp_gather(head_rows)
    up_all = at.dp_gather(up_rows).reshape(width, dp * units)
    back_all = at.dp_gather(join(down_weight, out_rows, (up_rows,)))

    gathered = head_all[:, seq * shard :, :].reshape(dp, seq, 8, 3 * span)
    bias_in, bias_out, bias_up, bias_down, gain_attn, shift_attn, gain_ff, shift_ff = (
        gathered[:, :, i, : v.shape[0]].reshape(-1).astype(full) for i, v in enumerate(vectors)
    )
    norms = jnp.stack([gain_attn, shift_attn, gain_ff, shift_ff], 0)

    rows = seq * seqs * block
    pieces = [p.reshape(-1, width) for p in tokens_all]
    in_bias_mine = jnp.swapaxes(
        pick(bias_in.reshape(3, seq, groups, lanes), rank, 1), 0, 1
    ).reshape(1, 3 * span)
    up_bias_mine = pick(bias_up.reshape(dp, seq, units), rank, 1).reshape(1, dp * units)

    cos_table, sin_table = rotary_tables(seq * block, lanes, head_dim)

    def run(pieces, *more):
        return project(
            place, pieces, head_all, in_bias_mine, norms, jnp.asarray(cos_table), jnp.asarray(sin_table),
            block, seqs, lanes, head_dim, seq * shard, rows, *more,
        )

    if seq == 4 and seqs == 1:
        earlier = run(pieces[:3])
        cot_near = at.seq_gather_near(after(cotangent, earlier[3]))
        x, normed_attn, normed_ff, qkv = run(pieces[3:], 3, tuple(earlier))
    else:
        x, normed_attn, normed_ff, qkv = run([jnp.concatenate(pieces, 0)])
        cot_near = at.seq_gather_near(cotangent)
    qkv = qkv.reshape(seq, seqs, block, 3 * span)
    exact, attended, lse = attend(place, qkv, pair, head_dim)
    attended = attended.reshape(rows, span)
    cot_all = at.seq_gather_far(cot_near, attended)

    active, slope = expand(normed_ff, up_all, up_bias_mine, block, (attended,))

    pieces = [p.reshape(-1, width) for p in cot_all]
    if seq != 4 or seqs != 1:
        pieces = [jnp.concatenate(pieces, 0)]
    out_part, cot, attended_grad, hidden_grad, up_bias_sum = turnabout(
        attended, active, slope, back_all, pieces, block, units
    )
    if len(out_part) == 1:
        out_part = out_part[0].reshape(seq, seqs * block, width)
    out_near = [at.seq_swap(out_part[k], k) for k in range(1, seq)]

    out_grad = lax.optimization_barrier(contract(attended, cot, 0, 0).astype(low))
    out_grads = at.dp_reduce(out_grad.reshape(dp, shard, width))
    if dp * units == width:
        unit_grads = outer([(active, cot), (normed_ff, hidden_grad)], dp, 2)
    else:
        down_grad = contract(active, cot, 0, 0).astype(low)
        up_grad = contract(normed_ff, hidden_grad, 0, 0).astype(low)
        unit_grads = jnp.concatenate(
            [down_grad.reshape(dp, units, width), up_grad.reshape(dp, seq * shard * dp * units // width, width)], 1
        )
    back_wait = (unit_grads, out_grad)
    unit_sum_grads = at.dp_reduce(unit_grads)

    tables = [jnp.asarray(t.reshape(seq, block, lanes)) for t in (cos_table, sin_table)]
    mixed_grad = attend_back(
        place, qkv, exact, attended_grad.reshape(seq, seqs, block, span), lse, *tables, pair, head_dim, back_wait
    )
    mixed_grad = mixed_grad.reshape(rows, 3 * span)
    in_grad = lax.optimization_barrier(contract(normed_attn, mixed_grad, 0, 0).astype(low))
    in_grad = in_grad.reshape(dp, seq * shard, 3 * span)
    wait = (out_grads,)
    last = (seq - 1) * seqs
    weights = (head_all, up_all, norms)
    far_grad, far_sums = unproject(x, mixed_grad, hidden_grad, *weights, block, last, seqs, wait)
    in_ready = after_big(in_grad, unit_sum_grads)
    in_grads = at.dp_reduce(in_ready)
    near_grad, near_sums = unproject(x, mixed_grad, hidden_grad, *weights, block, seqs, last - seqs, (far_grad, in_ready))
    own_grad, own_sums = unproject(x, mixed_grad, hidden_grad, *weights, block, 0, seqs, (near_grad,))
    norm_sums = far_sums + near_sums + own_sums
    near_grad = near_grad.reshape(seq - 2, seqs, block, width)
    _, unit_near = reduce_steps(
        at, far_grad.reshape(seqs, block, width), lambda: [near_grad[k] for k in range(seq - 2)]
    )
    out_sum = out_part[0].astype(full) + sum(a.astype(full) for a in out_near)
    output = tokens.astype(full) + out_sum.reshape(tokens.shape) + (bias_out + bias_down)
    output = output.astype(low)
    in_bias_sum = jnp.sum(mixed_grad.astype(full), axis=0).reshape(groups, 3, lanes)
    in_bias_sum = jnp.swapaxes(in_bias_sum, 0, 1).reshape(3, 1, span)
    in_bias_sum = lax.dynamic_update_slice_in_dim(jnp.zeros((3, seq, span), full), in_bias_sum, rank, 1)
    up_bias_sum = up_bias_sum.reshape(dp, 1, units)
    up_bias_sum = lax.dynamic_update_slice_in_dim(jnp.zeros((dp, seq, units), full), up_bias_sum, rank, 1)
    out_bias_sum = jnp.sum(cotangent.astype(full), axis=(0, 1))
    in_bias_sum = in_bias_sum.reshape(3 * width)
    small = [
        in_bias_sum[: 2 * width],
        in_bias_sum[2 * width :],
        out_bias_sum,
        up_bias_sum,
        norm_sums[0],
        norm_sums[1],
        norm_sums[2],
        norm_sums[3],
    ]
    small = jnp.concatenate([v.reshape(dp, seq, -1) for v in small], 2)
    lengths = [3 * shard - shard, shard, shard, units, shard, shard, shard, shard]
    edges = np.cumsum([0] + lengths)

    down_final = unit_sum_grads[:units].astype(full)
    up_final = unit_sum_grads[units:].reshape(seq, shard, dp * units)
    up_moves = [(d * units, d * seq * units, units, units) for d in range(dp)]
    up_final = hand(place, at.seq_exchange(lambda spot: pick(up_final, spot, 0)), up_moves)
    out_final = at.from_heads(out_grads).astype(full)
    in_split = in_grads.reshape(seq, shard, 3 * span)
    in_moves = [
        ((g * 3 + kind) * lanes, kind * width + g * lanes, span, lanes) for g in range(groups) for kind in range(3)
    ]
    in_final = hand(place, at.seq_exchange(lambda spot: pick(in_split, spot, 0)), in_moves)
    total = at.small_reduce(small)
    flat = [a.reshape(-1, width) for a in (tokens, cotangent, own_grad)]
    if len(unit_near) == 2:
        others = [a.reshape(-1, width) for a in unit_near]
    else:
        others = [sum(a.astype(full) for a in unit_near).reshape(-1, width), jnp.zeros_like(flat[0])]
    token_grad = finish(*flat, *others, (output, total, up_final)).reshape(seqs, block, width)
    (query_key_bias, value_bias, out_bias, up_bias_grad, *norm_grads) = [
        total[edges[i] : edges[i + 1]] for i in range(8)
    ]
    return (
        output,
        token_grad,
        in_final,
        query_key_bias,
        value_bias,
        out_final,
        out_bias,
        up_final,
        up_bias_grad,
        down_final,
        out_bias,
        *norm_grads,
    )


def solution(mesh):
    rows = P(("dp", "seq"), None)
    flat = P(("dp", "seq"))
    held = P("dp", "seq", None)
    return jax.shard_map(
        on_device,
        mesh=mesh,
        in_specs=(held, rows, flat, rows, flat, rows, flat, rows, flat, flat, flat, flat, flat, held),
        out_specs=(held, held, rows, flat, flat, rows, flat, rows, flat, rows, flat, flat, flat, flat, flat),
        check_vma=False,
    )
```

```python
import functools
import math

import jax
import jax.numpy as jnp
import numpy as np
from jax import lax
from jax.experimental import pallas as pl
from jax.experimental.pallas import tpu as pltpu
from jax.sharding import PartitionSpec as P

HEADS = 16
ROT = 16

norm_eps = 1e-05
masked_score = -1e30
low = jnp.bfloat16
full = jnp.float32
kernel_memory = 56 * 1024 * 1024


def place_at(pieces, spots, axis):
    count = len(pieces)
    shape = list(pieces[0].shape)
    shape.insert(axis, count)
    held = jnp.zeros(shape, pieces[0].dtype)
    for piece, spot in zip(pieces, spots):
        held = lax.dynamic_update_index_in_dim(held, piece, spot, axis)
    return held


def pick(array, spot, axis):
    return lax.dynamic_index_in_dim(array, spot, axis, keepdims=False)


def effort(micros):
    return pl.CostEstimate(flops=int(micros * 1.1e9), bytes_accessed=1, transcendentals=0)


anywhere = pl.BlockSpec(memory_space=pl.ANY)


def pass_kernel(*refs):
    del refs


def after_big(array, *others):
    return pl.pallas_call(
        pass_kernel,
        in_specs=[anywhere] * (1 + len(others)),
        out_specs=anywhere,
        out_shape=jax.ShapeDtypeStruct(array.shape, array.dtype),
        input_output_aliases={0: 0},
        name="after_big",
    )(array, *others)


def join_kernel(first, second, *refs):
    rows = first.shape[0]
    refs[-1][:rows, :] = first[...]
    refs[-1][rows:, :] = second[...]


def join(first, second, wait):
    vmem = pl.BlockSpec(memory_space=pltpu.VMEM)
    return pl.pallas_call(
        join_kernel,
        in_specs=[vmem, vmem] + [anywhere] * len(wait),
        out_specs=vmem,
        out_shape=jax.ShapeDtypeStruct((first.shape[0] + second.shape[0], first.shape[1]), first.dtype),
        compiler_params=pltpu.CompilerParams(vmem_limit_bytes=kernel_memory),
        name="join",
    )(first, second, *wait)


def after_kernel(source, *refs):
    refs[-1][...] = source[...]


def after(array, *others):
    vmem = pl.BlockSpec(memory_space=pltpu.VMEM)
    return pl.pallas_call(
        after_kernel,
        in_specs=[vmem] + [anywhere] * len(others),
        out_specs=vmem,
        out_shape=jax.ShapeDtypeStruct(array.shape, array.dtype),
        compiler_params=pltpu.CompilerParams(vmem_limit_bytes=kernel_memory),
        name="after",
    )(array, *others)


def chosen_units(ref, rank, ranks, units):
    runs = ref.shape[1] // (ranks * units)
    parts = []
    for run in range(runs):
        first = run * ranks * units
        if units % 128 == 0:
            parts.append(ref[:, pl.ds(pl.multiple_of(first + rank * units, 128), units)])
        else:
            whole = ref[:, first : first + ranks * units]
            part = jnp.zeros((ref.shape[0], units), ref.dtype)
            for r in range(ranks):
                part = jnp.where(rank == r, whole[:, r * units : (r + 1) * units], part)
            parts.append(part)
    return jnp.concatenate(parts, 1)


def deal_kernel(ranks, groups, vectors, units, place, in_ref, up_ref, *refs):
    shard, columns = in_ref.shape
    width = columns // 3
    span = width // ranks
    lanes = span // groups
    for k in range(ranks):
        rank = place[0] ^ k
        dealt = refs[vectors + k]
        dealt[:shard, 3 * span :] = jnp.zeros((shard, span), low)

        def part(start):
            first = start + rank * span
            if span % 128 == 0:
                return in_ref[:, pl.ds(pl.multiple_of(first, 128), span)]
            whole = in_ref[:, start : start + width]
            chosen = jnp.zeros((shard, span), low)
            for r in range(ranks):
                chosen = jnp.where(rank == r, whole[:, r * span : (r + 1) * span], chosen)
            return chosen

        for kind in range(3):
            mine = part(kind * width)
            for group in range(groups):
                target = (group * 3 + kind) * lanes
                dealt[:shard, target : target + lanes] = mine[:, group * lanes : (group + 1) * lanes]
        dealt[shard + 16 :, :] = chosen_units(up_ref, rank, ranks, units)
        dealt[shard : shard + 16, :] = jnp.zeros((16, 4 * span), low)
        for i, ref in enumerate(refs[:vectors]):
            dealt[shard + i : shard + i + 1, : ref.shape[1]] = ref[...]


def deal(place, input_weight, up_weight, vectors, ranks, groups, units):
    shard, columns = input_weight.shape
    arrays = [input_weight, up_weight] + [v[None] for v in vectors]
    shape = (2 * shard + 16, 4 * columns // (3 * ranks))
    vmem = pl.BlockSpec(memory_space=pltpu.VMEM)
    return pl.pallas_call(
        functools.partial(deal_kernel, ranks, groups, len(vectors), units),
        in_specs=[pl.BlockSpec(memory_space=pltpu.SMEM)] + [vmem] * len(arrays),
        out_specs=[vmem] * ranks,
        out_shape=[jax.ShapeDtypeStruct(shape, low)] * ranks,
        compiler_params=pltpu.CompilerParams(vmem_limit_bytes=kernel_memory),
        name="deal",
    )(place, *arrays)


def gather_heads_kernel(count, shard, place, *refs):
    out, units = refs[count:]
    columns = out.shape[1]
    for k in range(count):
        rank = place[0] ^ k
        if shard % 16 == 0:
            here = pl.ds(pl.multiple_of(rank * shard, 16), shard)
            out[here, :] = refs[k][:shard, :columns]
            units[here, :] = refs[k][shard + 16 :, :]
        else:
            for r in range(count):

                @pl.when(rank == r)
                def _(r=r, k=k):
                    out[r * shard : (r + 1) * shard, :] = refs[k][:shard, :columns]
                    units[r * shard : (r + 1) * shard, :] = refs[k][shard + 16 :, :]

    vectors = []
    for r in range(count):
        mine = jnp.zeros((8, columns), full)
        for k in range(count):
            rows = refs[k][shard : shard + 16, :columns].astype(full)[:8]
            mine = jnp.where((place[0] ^ k) == r, rows, mine)
        vectors.append(mine)
    out[count * shard :, :] = jnp.concatenate(vectors, 0).astype(low)


def gather_heads(place, pieces, shard):
    count = len(pieces)
    wide = pieces[0].shape[1]
    vmem = pl.BlockSpec(memory_space=pltpu.VMEM)
    return pl.pallas_call(
        functools.partial(gather_heads_kernel, count, shard),
        in_specs=[pl.BlockSpec(memory_space=pltpu.SMEM)] + [vmem] * count,
        out_specs=[vmem, vmem],
        out_shape=[
            jax.ShapeDtypeStruct((count * shard + count * 8, wide // 4 * 3), low),
            jax.ShapeDtypeStruct((count * shard, wide), low),
        ],
        compiler_params=pltpu.CompilerParams(vmem_limit_bytes=kernel_memory),
        name="gather_heads",
    )(place, *pieces)


def cut_kernel(x_ref, y_ref, *refs):
    first, second = refs[-2:]
    first[...] = x_ref[...]
    second[...] = y_ref[...]


def cut(x, y, wait):
    seqs, block, width = x.shape
    half = (seqs, block // 2, width)
    return pl.pallas_call(
        cut_kernel,
        grid=(1,),
        in_specs=[pl.BlockSpec(half, lambda i: (0, 0, 0)), pl.BlockSpec(half, lambda i: (0, 1, 0))]
        + [anywhere] * len(wait),
        out_specs=[pl.BlockSpec(half, lambda i: (0, 0, 0))] * 2,
        out_shape=[jax.ShapeDtypeStruct(half, x.dtype)] * 2,
        compiler_params=pltpu.CompilerParams(vmem_limit_bytes=kernel_memory),
        name="cut",
    )(x, y, *wait)


def lay_columns_kernel(count, place, *refs):
    out = refs[count]
    span = refs[0].shape[1]
    for k in range(count):
        rank = place[0] ^ k
        if span % 128 == 0:
            out[:, pl.ds(pl.multiple_of(rank * span, 128), span)] = refs[k][...]
        else:
            for r in range(count):

                @pl.when(rank == r)
                def _(r=r, k=k):
                    out[:, r * span : (r + 1) * span] = refs[k][...]


def lay_columns(place, pieces):
    count = len(pieces)
    rows, span = pieces[0].shape
    vmem = pl.BlockSpec(memory_space=pltpu.VMEM)
    return pl.pallas_call(
        functools.partial(lay_columns_kernel, count),
        in_specs=[pl.BlockSpec(memory_space=pltpu.SMEM)] + [vmem] * count,
        out_specs=vmem,
        out_shape=jax.ShapeDtypeStruct((rows, count * span), pieces[0].dtype),
        compiler_params=pltpu.CompilerParams(vmem_limit_bytes=kernel_memory),
        name="lay_columns",
    )(place, *pieces)


def lay_kernel(count, place, *refs):
    out = refs[count]
    for k in range(count):
        out[place[0] ^ k] = refs[k][...]


def lay(place, pieces):
    count = len(pieces)
    shape = (count,) + pieces[0].shape
    return pl.pallas_call(
        functools.partial(lay_kernel, count),
        grid_spec=pltpu.PrefetchScalarGridSpec(
            num_scalar_prefetch=1,
            grid=(1,),
            in_specs=[pl.BlockSpec(p.shape, lambda i, place, n=p.ndim: (0,) * n) for p in pieces],
            out_specs=pl.BlockSpec(shape, lambda i, place: (0,) * len(shape)),
        ),
        out_shape=jax.ShapeDtypeStruct(shape, pieces[0].dtype),
        compiler_params=pltpu.CompilerParams(vmem_limit_bytes=kernel_memory),
        name="lay",
    )(place, *pieces)


class Layout:
    def __init__(self):
        self.dp = lax.axis_size("dp")
        self.seq = lax.axis_size("seq")
        self.rank = lax.axis_index("seq")

    def seq_swap(self, array, k):
        return lax.ppermute(array, "seq", [(i, i ^ k) for i in range(self.seq)])

    def to_heads(self, array):
        pairs = [(f, (f % self.dp) * self.seq + f // self.dp) for f in range(self.dp * self.seq)]
        return lax.ppermute(array, ("dp", "seq"), pairs)

    def from_heads(self, array):
        pairs = [((f % self.dp) * self.seq + f // self.dp, f) for f in range(self.dp * self.seq)]
        return lax.ppermute(array, ("dp", "seq"), pairs)

    def seq_exchange(self, piece_for):
        return [piece_for(self.rank)] + [
            self.seq_swap(piece_for(self.rank ^ k), k) for k in range(1, self.seq)
        ]

    def seq_trade(self, array, place):
        return lay(place, self.seq_exchange(lambda spot: pick(array, spot, 0)))

    def seq_spots(self):
        return [self.rank ^ k for k in range(self.seq)]

    def seq_gather_direct(self, array):
        return [array] + [self.seq_swap(array, k) for k in range(1, self.seq)]

    def seq_gather(self, array):
        if self.seq != 4:
            return self.seq_gather_direct(array)
        return self.seq_gather_far(self.seq_gather_near(array))

    def seq_gather_near(self, array):
        if self.seq != 4:
            return self.seq_gather_direct(array)
        return [array, self.seq_swap(array, 1), self.seq_swap(array, 2)]

    def seq_gather_far(self, near, *wait):
        if self.seq != 4:
            return near
        first, second = cut(near[1], near[2], wait)
        return near + [self.seq_swap(first, 2), self.seq_swap(second, 1)]

    def seq_reduce_near(self, parts, far):
        half = parts[0].shape[1] // 2
        for_x, for_y = (a.astype(full) for a in far)
        p1, p2 = parts
        p1 = jnp.concatenate([p1[:, :half], (p1[:, half:].astype(full) + for_x).astype(low)], 1)
        p2 = jnp.concatenate([(p2[:, :half].astype(full) + for_y).astype(low), p2[:, half:]], 1)
        return self.seq_swap(p1, 1), self.seq_swap(p2, 2)

    def seq_turnover(self, array):
        return lax.all_to_all(array, "seq", 0, 0, tiled=True)

    def z_turn(self, array, k):
        return lax.ppermute(array, "dp", [(i, (i + k) % self.dp) for i in range(self.dp)])

    def small_reduce(self, array):
        array = sum(self.seq_exchange(lambda spot: pick(array, spot, 1)))
        cores = 2 if self.dp % 2 == 0 else 1
        here = lax.axis_index("dp")
        core, z = here % cores, here // cores
        line = self.dp // cores
        pairs = array.reshape((line, cores) + array.shape[1:])
        if cores == 2:
            swap = [(i, i ^ 1) for i in range(self.dp)]
            array = pick(pairs, core, 1) + lax.ppermute(pick(pairs, 1 - core, 1), "dp", swap)
        else:
            array = pairs[:, 0]
        total = pick(array, z, 0)
        for k in range(1, line):
            total = total + self.z_turn(pick(array, (z + k) % line, 0), k * cores)
        return total

    def dp_gather(self, array):
        return lax.all_gather(array, "dp", axis=0, tiled=False)

    def dp_reduce(self, array):
        return lax.psum_scatter(array, "dp", scatter_dimension=0, tiled=False)


def rotary_tables(length, lanes, head_dim):
    half = ROT // 2
    exponent = -np.arange(0, ROT, 2, dtype=np.float32) / np.float32(ROT)
    frequency = np.float32(10000.0) ** exponent
    phase = np.arange(length, dtype=np.float32)[:, None] * frequency[None, :]
    cosine = np.ones((length, head_dim), np.float32)
    sine = np.zeros((length, head_dim), np.float32)
    cosine[:, :half] = cosine[:, half:ROT] = np.cos(phase)
    sine[:, :half] = -np.sin(phase)
    sine[:, half:ROT] = np.sin(phase)
    copies = lanes // head_dim
    return np.tile(cosine, (1, copies)), np.tile(sine, (1, copies))


def roll_lanes(x, shift):
    size = x.shape[-1]
    if size % 128 == 0:
        return pltpu.roll(x, shift % size, x.ndim - 1)
    return jnp.roll(x, shift, -1)


def turn(x, cosine, sine, head_dim):
    half = ROT // 2
    lane = lax.broadcasted_iota(jnp.int32, x.shape, 1) % head_dim
    swapped = jnp.where(lane < half, roll_lanes(x, -half), roll_lanes(x, half))
    return x * cosine + swapped * sine


def normalised(x):
    mean = jnp.mean(x, axis=-1, keepdims=True)
    centered = x - mean
    variance = jnp.mean(centered * centered, axis=-1, keepdims=True)
    rstd = lax.rsqrt(variance + norm_eps)
    return centered * rstd, rstd


def project_kernel(head_dim, lanes, shard, columns, stacked, count, place, head_ref, bias_ref, norms_ref, cos_ref, sin_ref, *refs):
    pieces, (x_out, attn_ref, ff_ref, qkv_ref, weight_ref) = refs[:count], refs[-5:]
    block, width = x_out.shape
    step = pl.program_id(0)

    @pl.when(step == 0)
    def _():
        weight_ref[...] = head_ref[:, :shard, :columns].reshape(width, columns)

    if stacked:
        x_out[...] = pieces[0][...]
    else:
        first = 0
        for piece in pieces:
            rows = piece.shape[0]
            inside = first % block

            @pl.when(step == first // block)
            def _(piece=piece, inside=inside, rows=rows):
                x_out[inside : inside + rows, :] = piece[...]

            first += rows
    unit, _ = normalised(x_out[...].astype(full))
    normed = (unit * norms_ref[0:1, :] + norms_ref[1:2, :]).astype(low)
    attn_ref[...] = normed
    ff_ref[...] = (unit * norms_ref[2:3, :] + norms_ref[3:4, :]).astype(low)
    mixed = jnp.dot(normed, weight_ref[...], preferred_element_type=full) + bias_ref[...]
    cosine, sine = cos_ref[...], sin_ref[...]
    for group in range(columns // lanes):
        span = slice(group * lanes, (group + 1) * lanes)
        part = mixed[:, span]
        if group % 3 < 2:
            part = turn(part, cosine, sine, head_dim)
        qkv_ref[:, span] = part.astype(low)


def project(place, pieces, head, bias, norms, cosine, sine, block, seqs, lanes, head_dim, shard, rows, start=0, earlier=()):
    stacked = len(pieces) == 1
    width = pieces[0].shape[1]
    columns = bias.shape[1]
    whole = lambda i, place: (0, 0)
    step = lambda i, place: (i + start, 0)
    spot = lambda i, place: (((i + start) // seqs) ^ place[0], 0)
    if stacked:
        piece_specs = [pl.BlockSpec((block, width), step)]
    else:
        piece_specs = [pl.BlockSpec(p.shape, whole) for p in pieces]
    return pl.pallas_call(
        functools.partial(project_kernel, head_dim, lanes, shard, columns, stacked, len(pieces)),
        grid_spec=pltpu.PrefetchScalarGridSpec(
            num_scalar_prefetch=1,
            grid=(sum(p.shape[0] for p in pieces) // block,),
            in_specs=[
                pl.BlockSpec(head.shape, lambda i, place: (0, 0, 0)),
                pl.BlockSpec((1, columns), whole),
                pl.BlockSpec((4, width), whole),
                pl.BlockSpec((block, lanes), spot),
                pl.BlockSpec((block, lanes), spot),
            ]
            + piece_specs
            + [anywhere] * len(earlier),
            out_specs=[
                pl.BlockSpec((block, width), step),
                pl.BlockSpec((block, width), step),
                pl.BlockSpec((block, width), step),
                pl.BlockSpec((block, columns), step),
            ],
            scratch_shapes=[pltpu.VMEM((width, columns), low)],
        ),
        out_shape=[
            jax.ShapeDtypeStruct((rows, width), low),
            jax.ShapeDtypeStruct((rows, width), low),
            jax.ShapeDtypeStruct((rows, width), low),
            jax.ShapeDtypeStruct((rows, columns), low),
        ],
        input_output_aliases={6 + len(pieces) + i: i for i in range(len(earlier))},
        compiler_params=pltpu.CompilerParams(vmem_limit_bytes=kernel_memory),
        cost_estimate=effort(12 * sum(p.shape[0] for p in pieces) / 2048),
        name="project",
    )(place, head, bias, norms, cosine, sine, *pieces, *earlier)


def contract(a, b, da, db):
    return lax.dot_general(a, b, (((da,), (db,)), ((), ())), preferred_element_type=full)


def head_lanes(x, head, pair, head_dim):
    if pair == 1:
        return x
    lane = lax.broadcasted_iota(jnp.int32, x.shape, 1)
    inside = (lane >= head * head_dim) & (lane < (head + 1) * head_dim)
    return jnp.where(inside, x, jnp.zeros_like(x))


def attend_kernel(pair, head_dim, place, qkv_ref, exact_ref, low_ref, lse_ref):
    count, block, lanes3 = qkv_ref.shape
    lanes = lanes3 // 3
    scale = 1.0 / math.sqrt(head_dim)
    s = place[0]
    row = lax.broadcasted_iota(jnp.int32, (block, block), 0)
    column = lax.broadcasted_iota(jnp.int32, (block, block), 1)
    for i in range(count):
        here = i ^ s
        query = qkv_ref[here, :, 0:lanes] * jnp.asarray(scale, low)
        joined = jnp.zeros((block, lanes), full)
        for head in range(pair):
            mine = head_lanes(query, head, pair, head_dim)
            scores = []
            for j in range(i + 1):
                part = contract(mine, qkv_ref[j ^ s, :, lanes : 2 * lanes], 1, 1)
                if j == i:
                    part = jnp.where(column <= row, part, masked_score)
                scores.append(part)
            top = functools.reduce(jnp.maximum, scores)
            top = jnp.max(top, axis=-1, keepdims=True)
            total = None
            update = None
            for j in range(i + 1):
                weights = jnp.exp(scores[j] - top)
                term = jnp.dot(
                    weights.astype(low), qkv_ref[j ^ s, :, 2 * lanes :], preferred_element_type=full
                )
                update = term if update is None else update + term
                total = weights if total is None else total + weights
            total = jnp.sum(total, axis=-1, keepdims=True)
            joined = joined + head_lanes(update / total, head, pair, head_dim)
            lse = jnp.broadcast_to(top + jnp.log(total), (block, 128))
            lse_ref[here, head : head + 1, :] = jnp.transpose(lse)[0:1, :]
        exact_ref[here] = joined
        low_ref[here] = joined.astype(low)


def attend(place, qkv, pair, head_dim):
    count, seqs, block, columns = qkv.shape
    lanes = pair * head_dim
    groups = columns // (3 * lanes)
    spec = lambda width: pl.BlockSpec((count, None, block, width), lambda b, g, place: (0, b, 0, g))
    return pl.pallas_call(
        functools.partial(attend_kernel, pair, head_dim),
        grid_spec=pltpu.PrefetchScalarGridSpec(
            num_scalar_prefetch=1,
            grid=(seqs, groups),
            in_specs=[spec(3 * lanes)],
            out_specs=[
                spec(lanes),
                spec(lanes),
                pl.BlockSpec((count, None, None, pair, block), lambda b, g, place: (0, b, g, 0, 0)),
            ],
        ),
        out_shape=[
            jax.ShapeDtypeStruct((count, seqs, block, groups * lanes), full),
            jax.ShapeDtypeStruct((count, seqs, block, groups * lanes), low),
            jax.ShapeDtypeStruct((count, seqs, groups, pair, block), full),
        ],
        compiler_params=pltpu.CompilerParams(vmem_limit_bytes=kernel_memory),
        cost_estimate=effort(18 * seqs * groups / 2),
        name="attend",
    )(place, qkv)


def attend_back_kernel(pair, head_dim, place, qkv_ref, exact_ref, grad_ref, lse_ref, cos_ref, sin_ref, *refs):
    out_ref, key_ref, value_ref = refs[-3:]
    count, block, lanes3 = qkv_ref.shape
    lanes = lanes3 // 3
    scale = 1.0 / math.sqrt(head_dim)
    s = place[0]
    row = lax.broadcasted_iota(jnp.int32, (block, block), 0)
    column = lax.broadcasted_iota(jnp.int32, (block, block), 1)
    key_ref[...] = jnp.zeros_like(key_ref)
    value_ref[...] = jnp.zeros_like(value_ref)

    def back(total, at):
        kept = total.astype(low).astype(full)
        return turn(kept, cos_ref[at], -sin_ref[at], head_dim).astype(low)

    for i in range(count):
        here = i ^ s
        query = qkv_ref[here, :, 0:lanes] * jnp.asarray(scale, low)
        grad = grad_ref[here]
        product = exact_ref[here] * grad.astype(full)
        joined = jnp.zeros((block, lanes), full)
        for head in range(pair):
            mine = head_lanes(query, head, pair, head_dim)
            mine_grad = head_lanes(grad, head, pair, head_dim)
            delta = jnp.sum(
                jnp.transpose(head_lanes(product, head, pair, head_dim)), axis=0, keepdims=True
            )
            lse = lse_ref[here, head : head + 1, :]
            update = None
            for j in range(i + 1):
                there = j ^ s
                key = qkv_ref[there, :, lanes : 2 * lanes]
                value = qkv_ref[there, :, 2 * lanes :]
                scores = contract(key, mine, 1, 1)
                if j == i:
                    scores = jnp.where(row <= column, scores, masked_score)
                probs = jnp.exp(scores - lse)
                prob_grad = contract(value, mine_grad, 1, 1)
                score_grad = (probs * (prob_grad - delta)).astype(low)
                value_ref[j] += jnp.dot(probs.astype(low), mine_grad, preferred_element_type=full)
                key_ref[j] += jnp.dot(score_grad, mine, preferred_element_type=full)
                term = contract(score_grad, key, 0, 0)
                update = term if update is None else update + term
            joined = joined + head_lanes(update, head, pair, head_dim)
        out_ref[here, :, 0:lanes] = back(joined * scale, i)
    for j in range(count):
        there = j ^ s
        out_ref[there, :, lanes : 2 * lanes] = back(key_ref[j], j)
        out_ref[there, :, 2 * lanes :] = value_ref[j].astype(low)


def attend_back(place, qkv, exact, grad, lse, cosine, sine, pair, head_dim, wait):
    count, seqs, block, columns = qkv.shape
    lanes = pair * head_dim
    groups = columns // (3 * lanes)
    spec = lambda width: pl.BlockSpec((count, None, block, width), lambda b, g, place: (0, b, 0, g))
    table = pl.BlockSpec((count, block, lanes), lambda b, g, place: (0, 0, 0))
    return pl.pallas_call(
        functools.partial(attend_back_kernel, pair, head_dim),
        grid_spec=pltpu.PrefetchScalarGridSpec(
            num_scalar_prefetch=1,
            grid=(seqs, groups),
            in_specs=[
                spec(3 * lanes),
                spec(lanes),
                spec(lanes),
                pl.BlockSpec((count, None, None, pair, block), lambda b, g, place: (0, b, g, 0, 0)),
                table,
                table,
            ]
            + [anywhere] * len(wait),
            out_specs=spec(3 * lanes),
            scratch_shapes=[
                pltpu.VMEM((count, block, lanes), full),
                pltpu.VMEM((count, block, lanes), full),
            ],
        ),
        out_shape=jax.ShapeDtypeStruct(qkv.shape, low),
        compiler_params=pltpu.CompilerParams(vmem_limit_bytes=kernel_memory),
        cost_estimate=effort(33 * seqs * groups / 2),
        name="attend_back",
    )(place, qkv, exact, grad, lse, cosine, sine, *wait)


def expand_kernel(x_ref, weight_ref, bias_ref, *refs):
    active_ref, slope_ref = refs[-2:]
    hidden = jnp.dot(x_ref[...], weight_ref[...], preferred_element_type=full) + bias_ref[...]
    tail = 0.5 * (1.0 + lax.erf(hidden * np.float32(math.sqrt(0.5))))
    bell = jnp.exp(-0.5 * hidden * hidden) * np.float32(1.0 / math.sqrt(2.0 * math.pi))
    active_ref[...] = (hidden * tail).astype(low)
    slope_ref[...] = (tail + hidden * bell).astype(low)


def expand(x, weight, bias, block, wait):
    rows, width = x.shape
    columns = weight.shape[1]
    whole = lambda i: (0, 0)
    step = lambda i: (i, 0)
    return pl.pallas_call(
        expand_kernel,
        grid=(rows // block,),
        in_specs=[
            pl.BlockSpec((block, width), step),
            pl.BlockSpec((width, columns), whole),
            pl.BlockSpec((1, columns), whole),
        ]
        + [anywhere] * len(wait),
        out_specs=[pl.BlockSpec((block, columns), step), pl.BlockSpec((block, columns), step)],
        out_shape=[jax.ShapeDtypeStruct((rows, columns), low)] * 2,
        compiler_params=pltpu.CompilerParams(vmem_limit_bytes=kernel_memory),
        cost_estimate=effort(12 * rows / 2048),
        name="expand",
    )(x, weight, bias, *wait)


def turnabout_kernel(stacked, count, units, attended_ref, active_ref, slope_ref, back_ref, *refs):
    pieces, parts = refs[:count], refs[count:-6]
    cot_ref, attended_grad_ref, hidden_grad_ref, sum_ref, down_ref, out_ref = refs[-6:]
    block, width = cot_ref.shape
    step = pl.program_id(0)

    @pl.when(step == 0)
    def _():
        down_ref[...] = back_ref[:, :units, :].reshape(down_ref.shape)
        out_ref[...] = back_ref[:, units:, :].reshape(out_ref.shape)

    down, out = down_ref[...], out_ref[...]
    part = jnp.dot(attended_ref[...], out, preferred_element_type=full)
    part = part + jnp.dot(active_ref[...], down, preferred_element_type=full)
    part = part.astype(low)
    if stacked:
        cot_ref[...] = pieces[0][...]
        parts[0][...] = part
    else:
        for k, ref in enumerate(parts):

            @pl.when(step == k)
            def _(ref=ref):
                ref[...] = part

        first = 0
        for piece in pieces:
            rows = piece.shape[0]
            inside = first % block

            @pl.when(step == first // block)
            def _(piece=piece, inside=inside, rows=rows):
                cot_ref[inside : inside + rows, :] = piece[...]

            first += rows
    cot = cot_ref[...]
    attended_grad_ref[...] = contract(cot, out, 1, 1).astype(low)
    hidden = (contract(cot, down, 1, 1) * slope_ref[...].astype(full)).astype(low)
    hidden_grad_ref[...] = hidden
    total = jnp.sum(hidden.astype(full), axis=0, keepdims=True)

    @pl.when(step == 0)
    def _():
        sum_ref[...] = total

    @pl.when(step > 0)
    def _():
        sum_ref[...] += total


def turnabout(attended, active, slope, back_weights, pieces, block, units):
    stacked = len(pieces) == 1
    rows, span = attended.shape
    columns, width = active.shape[1], back_weights.shape[2]
    whole = lambda i: (0, 0)
    step = lambda i: (i, 0)
    if stacked:
        piece_specs = [pl.BlockSpec((block, width), step)]
        part_specs = piece_specs
        part_shapes = [jax.ShapeDtypeStruct((rows, width), low)]
    else:
        piece_specs = [pl.BlockSpec(p.shape, whole) for p in pieces]
        part_specs = [pl.BlockSpec((block, width), whole)] * (rows // block)
        part_shapes = [jax.ShapeDtypeStruct((block, width), low)] * (rows // block)
    *parts, cot, attended_grad, hidden_grad, total = pl.pallas_call(
        functools.partial(turnabout_kernel, stacked, len(pieces), units),
        grid=(rows // block,),
        in_specs=[
            pl.BlockSpec((block, span), step),
            pl.BlockSpec((block, columns), step),
            pl.BlockSpec((block, columns), step),
            pl.BlockSpec(back_weights.shape, lambda i: (0, 0, 0)),
        ]
        + piece_specs,
        out_specs=part_specs
        + [
            pl.BlockSpec((block, width), step),
            pl.BlockSpec((block, span), step),
            pl.BlockSpec((block, columns), step),
            pl.BlockSpec((1, columns), whole),
        ],
        out_shape=part_shapes
        + [
            jax.ShapeDtypeStruct((rows, width), low),
            jax.ShapeDtypeStruct((rows, span), low),
            jax.ShapeDtypeStruct((rows, columns), low),
            jax.ShapeDtypeStruct((1, columns), full),
        ],
        scratch_shapes=[pltpu.VMEM((columns, width), low), pltpu.VMEM((span, width), low)],
        compiler_params=pltpu.CompilerParams(vmem_limit_bytes=kernel_memory),
        cost_estimate=effort(14 * rows / 2048),
        name="turnabout",
    )(attended, active, slope, back_weights, *pieces)
    return parts, cot, attended_grad, hidden_grad, total


def outer_kernel(count, *refs):
    out_ref = refs[2 * count]
    for which in range(count):

        @pl.when(pl.program_id(0) == which)
        def _(which=which):
            got = contract(refs[2 * which][...], refs[2 * which + 1][...], 0, 0)
            out_ref[...] = got.astype(low).reshape(out_ref.shape)


def outer(pairs, parts, halves):
    count = len(pairs)
    rows, columns = pairs[0][0].shape
    width = pairs[0][1].shape[1]
    units = columns // parts
    specs, arrays = [], []
    for which, (a, b) in enumerate(pairs):
        mine = lambda w, h, which=which: (0, jnp.where(w == which, h, jnp.where(w < which, 0, halves - 1)))
        specs += [pl.BlockSpec((rows, columns // halves), mine), pl.BlockSpec((rows, width), lambda w, h: (0, 0))]
        arrays += [a, b]
    return pl.pallas_call(
        functools.partial(outer_kernel, count),
        grid=(count, halves),
        in_specs=specs,
        out_specs=pl.BlockSpec((parts // halves, units, width), lambda w, h: (h, w, 0)),
        out_shape=jax.ShapeDtypeStruct((parts, count * units, width), low),
        compiler_params=pltpu.CompilerParams(vmem_limit_bytes=kernel_memory),
        cost_estimate=effort(5 * count * rows * columns * width / 2**31),
        name="outer",
    )(*arrays)


def hand_kernel(count, moves, place, *refs):
    out = refs[count]
    for k in range(count):
        rank = place[0] ^ k
        for source, target, stride, size in moves:
            piece = refs[k][:, source : source + size].astype(full)
            if size % 128 == 0 and stride % 128 == 0:
                out[:, pl.ds(pl.multiple_of(target + rank * stride, 128), size)] = piece
            else:
                for r in range(count):

                    @pl.when(rank == r)
                    def _(r=r, piece=piece, target=target, stride=stride, size=size):
                        out[:, target + r * stride : target + r * stride + size] = piece


def hand(place, pieces, moves, columns):
    count = len(pieces)
    rows = pieces[0].shape[0]
    vmem = pl.BlockSpec(memory_space=pltpu.VMEM)
    return pl.pallas_call(
        functools.partial(hand_kernel, count, moves),
        in_specs=[pl.BlockSpec(memory_space=pltpu.SMEM)] + [vmem] * count,
        out_specs=vmem,
        out_shape=jax.ShapeDtypeStruct((rows, columns), full),
        compiler_params=pltpu.CompilerParams(vmem_limit_bytes=kernel_memory),
        name="hand",
    )(place, *pieces)


def settle_kernel(count, *refs):
    total = refs[count][...]
    for ref in refs[:count]:
        total = total + ref[...].astype(full)
    refs[-1][...] = total.astype(low)


def settle(parts, bias, wait):
    rows, width = parts[0].shape
    block = rows // 4 if rows % 64 == 0 else rows
    spec = pl.BlockSpec((block, width), lambda i: (i, 0))
    return pl.pallas_call(
        functools.partial(settle_kernel, len(parts)),
        grid=(rows // block,),
        in_specs=[spec] * len(parts) + [pl.BlockSpec((1, width), lambda i: (0, 0))] + [anywhere] * len(wait),
        out_specs=spec,
        out_shape=jax.ShapeDtypeStruct((rows, width), low),
        compiler_params=pltpu.CompilerParams(vmem_limit_bytes=kernel_memory),
        cost_estimate=effort(3 * rows / 512),
        name="settle",
    )(*parts, bias, *wait)


def finish_kernel(x_ref, cot_ref, own_ref, first_ref, second_ref, *refs):
    unit, rstd = normalised(x_ref[...].astype(full))
    total = own_ref[...].astype(full) + first_ref[...].astype(full) + second_ref[...].astype(full)
    shift = jnp.mean(total, axis=-1, keepdims=True)
    tilt = jnp.mean(total * unit, axis=-1, keepdims=True)
    refs[-1][...] = (cot_ref[...].astype(full) + rstd * (total - shift - unit * tilt)).astype(low)


def finish(x, cot, own, first, second, wait):
    rows, width = x.shape
    block = rows // 4 if rows % 64 == 0 else rows
    spec = pl.BlockSpec((block, width), lambda i: (i, 0))
    return pl.pallas_call(
        finish_kernel,
        grid=(rows // block,),
        in_specs=[spec] * 5 + [anywhere] * len(wait),
        out_specs=spec,
        out_shape=jax.ShapeDtypeStruct((rows, width), low),
        compiler_params=pltpu.CompilerParams(vmem_limit_bytes=kernel_memory),
        cost_estimate=effort(3 * rows / 512),
        name="finish",
    )(x, cot, own, first, second, *wait)


def unproject_kernel(outs, x_ref, mixed_ref, hidden_ref, in_ref, up_ref, norms_ref, *refs):
    out_refs, sums_ref = refs[-1 - outs : -1], refs[-1]
    unit, _ = normalised(x_ref[...].astype(full))
    width, columns = x_ref.shape[1], mixed_ref.shape[1]
    in_weight = in_ref[:, : width // in_ref.shape[0], :columns].reshape(width, columns)
    attn = contract(mixed_ref[...], in_weight, 1, 1)
    ff = contract(hidden_ref[...], up_ref[...], 1, 1)
    result = (attn * norms_ref[0:1, :] + ff * norms_ref[2:3, :]).astype(low)
    part = result.shape[0] // outs
    for k, out_ref in enumerate(out_refs):
        out_ref[...] = result[k * part : (k + 1) * part]
    sums = [attn * unit, attn, ff * unit, ff]
    sums = jnp.concatenate([jnp.sum(a, axis=0, keepdims=True) for a in sums], 0)

    @pl.when(pl.program_id(0) == 0)
    def _():
        sums_ref[...] = sums

    @pl.when(pl.program_id(0) > 0)
    def _():
        sums_ref[...] += sums


def unproject(x, mixed, hidden, in_weight, up_weight, norms, block, first, count, wait, outs=1):
    rows, width = count * block, x.shape[1]
    whole = lambda i: (0, 0)
    step = lambda i: (i + first, 0)
    here = lambda i: (i, 0)
    return pl.pallas_call(
        functools.partial(unproject_kernel, outs),
        grid=(rows // block,),
        in_specs=[
            pl.BlockSpec((block, width), step),
            pl.BlockSpec((block, mixed.shape[1]), step),
            pl.BlockSpec((block, hidden.shape[1]), step),
            pl.BlockSpec(in_weight.shape, lambda i: (0, 0, 0)),
            pl.BlockSpec(up_weight.shape, whole),
            pl.BlockSpec((4, width), whole),
        ]
        + [anywhere] * len(wait),
        out_specs=[pl.BlockSpec((block // outs, width), here)] * outs + [pl.BlockSpec((4, width), whole)],
        out_shape=[jax.ShapeDtypeStruct((rows // outs, width), low)] * outs
        + [
            jax.ShapeDtypeStruct((4, width), full),
        ],
        compiler_params=pltpu.CompilerParams(vmem_limit_bytes=kernel_memory),
        cost_estimate=effort(18 * rows / 2048),
        name="unproject",
    )(x, mixed, hidden, in_weight, up_weight, norms, *wait)


def on_device(
    tokens,
    input_weight,
    input_bias,
    output_weight,
    output_bias,
    up_weight,
    up_bias,
    down_weight,
    down_bias,
    attention_gain,
    attention_shift,
    feedforward_gain,
    feedforward_shift,
    cotangent,
):
    at = Layout()
    dp, seq, rank = at.dp, at.seq, at.rank
    seqs, block, width = tokens.shape
    shard = input_weight.shape[0]
    units = down_weight.shape[0]
    head_dim = width // HEADS
    heads = HEADS // seq
    pair = 2 if heads % 2 == 0 else 1
    groups = heads // pair
    lanes = pair * head_dim
    span = heads * head_dim
    place = rank.astype(jnp.int32).reshape(1)

    vectors = (input_bias, output_bias, up_bias, down_bias, attention_gain, attention_shift, feedforward_gain, feedforward_shift)
    dealt = deal(place, input_weight, up_weight, vectors, seq, groups, units)
    head_rows, up_rows = gather_heads(
        place, [dealt[0]] + [at.seq_swap(dealt[k], k) for k in range(1, seq)], shard
    )
    out_rows = at.to_heads(output_weight)
    tokens_all = at.seq_gather(tokens)
    head_all = at.dp_gather(head_rows)
    up_all = at.dp_gather(up_rows).reshape(width, dp * units)
    back_all = at.dp_gather(join(down_weight, out_rows, (up_rows,)))

    gathered = head_all[:, seq * shard :, :].reshape(dp, seq, 8, 3 * span)
    bias_in, bias_out, bias_up, bias_down, gain_attn, shift_attn, gain_ff, shift_ff = (
        gathered[:, :, i, : v.shape[0]].reshape(-1).astype(full) for i, v in enumerate(vectors)
    )
    norms = jnp.stack([gain_attn, shift_attn, gain_ff, shift_ff], 0)

    rows = seq * seqs * block
    pieces = [p.reshape(-1, width) for p in tokens_all]
    in_bias_mine = jnp.swapaxes(
        pick(bias_in.reshape(3, seq, groups, lanes), rank, 1), 0, 1
    ).reshape(1, 3 * span)
    up_bias_mine = pick(bias_up.reshape(dp, seq, units), rank, 1).reshape(1, dp * units)

    cos_table, sin_table = rotary_tables(seq * block, lanes, head_dim)

    def run(pieces, *more):
        return project(
            place, pieces, head_all, in_bias_mine, norms, jnp.asarray(cos_table), jnp.asarray(sin_table),
            block, seqs, lanes, head_dim, seq * shard, rows, *more,
        )

    if seq == 4 and seqs == 1:
        earlier = run(pieces[:3])
        cot_near = at.seq_gather_near(after(cotangent, earlier[3]))
        x, normed_attn, normed_ff, qkv = run(pieces[3:], 3, tuple(earlier))
    else:
        x, normed_attn, normed_ff, qkv = run([jnp.concatenate(pieces, 0)])
        cot_near = at.seq_gather_near(cotangent)
    qkv = qkv.reshape(seq, seqs, block, 3 * span)
    exact, attended, lse = attend(place, qkv, pair, head_dim)
    attended = attended.reshape(rows, span)
    cot_all = at.seq_gather_far(cot_near, attended)

    active, slope = expand(normed_ff, up_all, up_bias_mine, block, (attended,))

    pieces = [p.reshape(-1, width) for p in cot_all]
    if seq != 4 or seqs != 1:
        pieces = [jnp.concatenate(pieces, 0)]
    out_part, cot, attended_grad, hidden_grad, up_bias_sum = turnabout(
        attended, active, slope, back_all, pieces, block, units
    )
    if len(out_part) == 1:
        out_part = out_part[0].reshape(seq, seqs * block, width)
    out_near = [at.seq_swap(out_part[k], k) for k in range(1, seq)]

    out_grad = lax.optimization_barrier(contract(attended, cot, 0, 0).astype(low))
    out_grads = at.dp_reduce(out_grad.reshape(dp, shard, width))
    if dp * units == width:
        unit_grads = outer([(active, cot), (normed_ff, hidden_grad)], dp, 2)
    else:
        down_grad = contract(active, cot, 0, 0).astype(low)
        up_grad = contract(normed_ff, hidden_grad, 0, 0).astype(low)
        unit_grads = jnp.concatenate(
            [down_grad.reshape(dp, units, width), up_grad.reshape(dp, seq * shard * dp * units // width, width)], 1
        )
    back_wait = (unit_grads, out_grad)
    unit_sum_grads = at.dp_reduce(unit_grads)

    tables = [jnp.asarray(t.reshape(seq, block, lanes)) for t in (cos_table, sin_table)]
    mixed_grad = attend_back(
        place, qkv, exact, attended_grad.reshape(seq, seqs, block, span), lse, *tables, pair, head_dim, back_wait
    )
    mixed_grad = mixed_grad.reshape(rows, 3 * span)
    in_grad = lax.optimization_barrier(contract(normed_attn, mixed_grad, 0, 0).astype(low))
    in_grad = in_grad.reshape(dp, seq * shard, 3 * span)
    wait = (out_grads, *out_near)
    last = (seq - 1) * seqs
    weights = (head_all, up_all, norms)
    halves = 2 if seq == 4 and seqs == 1 else 1
    *far_grad, far_sums = unproject(x, mixed_grad, hidden_grad, *weights, block, last, seqs, wait, halves)
    in_ready = after_big(in_grad, unit_sum_grads)
    in_grads = at.dp_reduce(in_ready)
    near_grad, near_sums = unproject(x, mixed_grad, hidden_grad, *weights, block, seqs, last - seqs, (far_grad[0], in_ready))
    own_grad, own_sums = unproject(x, mixed_grad, hidden_grad, *weights, block, 0, seqs, (near_grad,))
    norm_sums = far_sums + near_sums + own_sums
    near_grad = near_grad.reshape(seq - 2, seqs, block, width)
    others = [near_grad[k] for k in range(seq - 2)]
    if halves == 2:
        first, second = (a.reshape(seqs, block // 2, width) for a in far_grad)
        far = (at.seq_swap(second, 2), at.seq_swap(first, 1))
        unit_near = list(at.seq_reduce_near(others, far))
    else:
        others = others + [far_grad[0].reshape(seqs, block, width)]
        unit_near = [at.seq_swap(a, k + 1) for k, a in enumerate(others)]
    bias = (bias_out + bias_down).reshape(1, width)
    parts = [a.reshape(-1, width) for a in (tokens, out_part[0], *out_near)]
    output = settle(parts, bias, (own_grad,)).reshape(tokens.shape)

    in_bias_sum = jnp.sum(mixed_grad.astype(full), axis=0).reshape(groups, 3, lanes)
    in_bias_sum = jnp.swapaxes(in_bias_sum, 0, 1).reshape(3, 1, span)
    in_bias_sum = lax.dynamic_update_slice_in_dim(jnp.zeros((3, seq, span), full), in_bias_sum, rank, 1)
    up_bias_sum = up_bias_sum.reshape(dp, 1, units)
    up_bias_sum = lax.dynamic_update_slice_in_dim(jnp.zeros((dp, seq, units), full), up_bias_sum, rank, 1)
    out_bias_sum = jnp.sum(cotangent.astype(full), axis=(0, 1))
    in_bias_sum = in_bias_sum.reshape(3 * width)
    small = [
        in_bias_sum[: 2 * width],
        in_bias_sum[2 * width :],
        out_bias_sum,
        up_bias_sum,
        norm_sums[0],
        norm_sums[1],
        norm_sums[2],
        norm_sums[3],
    ]
    small = jnp.concatenate([v.reshape(dp, seq, -1) for v in small], 2)
    lengths = [3 * shard - shard, shard, shard, units, shard, shard, shard, shard]
    edges = np.cumsum([0] + lengths)

    down_final = unit_sum_grads[:units].astype(full)
    up_final = unit_sum_grads[units:].reshape(seq, shard, dp * units)
    out_final = at.from_heads(out_grads).astype(full)
    own = dp * units
    handed = jnp.concatenate([up_final, in_grads.reshape(seq, shard, 3 * span)], 2)
    pieces = at.seq_exchange(lambda spot: pick(handed, spot, 0))
    up_moves = [(d * units, d * seq * units, units, units) for d in range(dp)]
    in_moves = [
        (own + (g * 3 + kind) * lanes, kind * width + g * lanes, span, lanes) for g in range(groups) for kind in range(3)
    ]
    up_final = hand(place, pieces, up_moves, dp * seq * units)
    in_final = hand(place, pieces, in_moves, 3 * width)
    total = at.small_reduce(small)
    flat = [a.reshape(-1, width) for a in (tokens, cotangent, own_grad)]
    if len(unit_near) == 2:
        others = [a.reshape(-1, width) for a in unit_near]
    else:
        others = [sum(a.astype(full) for a in unit_near).reshape(-1, width), jnp.zeros_like(flat[0])]
    token_grad = finish(*flat, *others, (output, pieces[0])).reshape(seqs, block, width)
    (query_key_bias, value_bias, out_bias, up_bias_grad, *norm_grads) = [
        total[edges[i] : edges[i + 1]] for i in range(8)
    ]
    return (
        output,
        token_grad,
        in_final,
        query_key_bias,
        value_bias,
        out_final,
        out_bias,
        up_final,
        up_bias_grad,
        down_final,
        out_bias,
        *norm_grads,
    )


def solution(mesh):
    rows = P(("dp", "seq"), None)
    flat = P(("dp", "seq"))
    held = P("dp", "seq", None)
    return jax.shard_map(
        on_device,
        mesh=mesh,
        in_specs=(held, rows, flat, rows, flat, rows, flat, rows, flat, flat, flat, flat, flat, held),
        out_specs=(held, held, rows, flat, flat, rows, flat, rows, flat, rows, flat, flat, flat, flat, flat),
        check_vma=False,
    )
```
